32 devices in a mesh: groups: 2 (over x), attn: 4 (over y, core), ffn: 4 (over z).
Axes of the slice: x: 2, y: 2, z: 4, core: 2. Of those that a mesh axis runs over, the one named last changes fastest.
Arguments:
- queries: bfloat16 [256, 16384], P(('groups', 'attn'), 'ffn'), parts along dimension 0, may hold values from -37 to 37
- new_kv: bfloat16 [256, 512], P(('groups', 'attn')), parts along dimension 0, may hold values from -6 to 6
- cache_pool: bfloat16 [112, 256, 512], P(('groups', 'attn')), parts along dimension 0, may hold values from -6 to 6
- request_owner: int32 [256], P('groups'), parts along dimension 0, may hold values from 0 to 3, as said below
- block_req: int32 [8, 14], P('groups'), parts along dimension 0, may hold values from 0 to 128, as said below
- migrate: int32 [8, 4, 1], P('groups'), parts along dimension 0, may hold values from 0 to 14, as said below
- residual_rows: bfloat16 [256, 7168], P('groups', 'attn'), parts along dimension 0, may hold values from -6 to 6
- w_out: bfloat16 [16384, 7168], P('ffn', 'attn'), may hold values from -0.046875 to 0.046875
- w_gate: bfloat16 [7168, 18432], P('attn', 'ffn'), may hold values from -0.0625 to 0.0625
- w_up: bfloat16 [7168, 18432], P('attn', 'ffn'), may hold values from -0.0625 to 0.0625
- w_down: bfloat16 [18432, 7168], P('ffn', 'attn'), may hold values from -0.046875 to 0.046875
Outputs:
- attention: bfloat16 [256, 16384], P(('groups', 'attn'), 'ffn'), parts along dimension 0
- arrived: bfloat16 [24, 256, 512], P(('groups', 'attn')), parts along dimension 0
- ffn_out: bfloat16 [256, 7168], P(('groups', 'ffn'), 'attn'), parts along dimension 0
The draws below stay inside these ranges and needn't reach their ends.
There are 2 independent parts, one for each index of `groups`. The reference program is written for one: setup_inputs(seed, part) draws one part's arguments, and reference() takes and returns one part's arrays. A program takes and returns all parts, laid end to end along the dimension named above; an argument that names none is the same for every part. Nothing has to cross between parts.
Inputs may be any that keep to these rules, and one draw needn't show every extreme that they name: `request_owner`: each source device (requests i*32 to (i+1)*32 - 1) sends exactly 8 requests to each of four attention devices. `block_req`: A device's live pages come first and belong to requests that request_owner maps to that device; a device holds up to 14 live pages. `migrate`: A device moves only its own last live pages, each once; at most 3 pages arrive at one device.
All inputs are finite; a program needn't handle non-finite values.
Results may differ from the reference program's by a relative error of at most 0.0057.
Values may be sent and summed in bfloat16 or wider, within the bound.
No kernel may reach another device: no remote copies, remote signals or barrier semaphores. Data moves between devices by JAX's collectives and lax.ppermute only.
A program may use at most 192 MiB of HBM per device.

```python
import jax
import jax.numpy as jnp
from jax import lax

D = 7168
FF = 18432
HEADS = 64
HD = 256
BLK = 256
MPAIR = 1
REQ_DEV = 32
POOL = 14
CAP = 8
SLOTS = 32
REQ = 128
HEAVY = 2
LIGHT = 2
R_IN = 3
N_ATTN = 4


def layout(key):
    first, second, third, fourth = jax.random.split(key, 4)
    permuted = jax.random.permutation(first, N_ATTN).astype(jnp.int32)
    sources = jnp.arange(N_ATTN, dtype=jnp.int32)[:, None]
    row_keys = jax.random.split(fourth, N_ATTN)
    shuffled = jax.vmap(lambda row_key: jax.random.permutation(row_key, REQ_DEV))(row_keys).astype(jnp.int32)
    group_of = shuffled // CAP
    shift = jax.random.randint(second, (), 0, LIGHT).astype(jnp.int32)
    heavy_pick = permuted[(sources + group_of) % HEAVY]
    light_pick = permuted[HEAVY + (sources + shift + group_of) % LIGHT]
    request_owner = jnp.where(group_of < 2, heavy_pick, light_pick).reshape(-1).astype(jnp.int32)
    order = jnp.arange(REQ, dtype=jnp.int32)
    same = request_owner[None, :] == request_owner[:, None]
    rank_owned = jnp.sum(jnp.logical_and(same, order[None, :] < order[:, None]), axis=1).astype(jnp.int32)
    devices = jnp.arange(N_ATTN, dtype=jnp.int32)
    held = jnp.sum((request_owner[None, :] == devices[:, None]).astype(jnp.int32), axis=1)
    place = jnp.sum(jnp.where(permuted[None, :] == devices[:, None], jnp.arange(N_ATTN, dtype=jnp.int32)[None, :], 0), axis=1)
    light_len = jax.random.randint(third, (N_ATTN,), 2, 6).astype(jnp.int32)
    live = jnp.where(place < HEAVY, POOL, light_len).astype(jnp.int32)
    page_index = jnp.arange(POOL, dtype=jnp.int32)
    wanted = page_index[None, :] % jnp.maximum(held, 1)[:, None]
    hits = jnp.logical_and(request_owner[None, None, :] == devices[:, None, None], rank_owned[None, None, :] == wanted[:, :, None])
    chosen = jnp.argmax(hits, axis=2).astype(jnp.int32)
    block_req = jnp.where(page_index[None, :] < live[:, None], chosen, REQ).astype(jnp.int32)
    moves = jnp.full((N_ATTN, N_ATTN, MPAIR), POOL, jnp.int32)
    for heavy_rank in range(HEAVY):
        for light_rank in range(LIGHT):
            moves = moves.at[permuted[heavy_rank], permuted[HEAVY + light_rank], 0].set(POOL - LIGHT + light_rank)
    for light_rank in range(LIGHT):
        giver = permuted[HEAVY + light_rank]
        moves = moves.at[giver, permuted[HEAVY + (light_rank + 1) % LIGHT], 0].set(live[giver] - 1)
    return (request_owner, block_req, moves)


def cache_values(key):
    key = jax.random.fold_in(key, 101)
    first = jax.random.fold_in(key, 0)
    extent = (N_ATTN * POOL, BLK, 2 * HD)
    smooth = jnp.clip(jax.random.normal(first, extent, jnp.float32), -6.0, 6.0)
    values = smooth
    second_key = values[:, 1:2, :HD]
    return values.at[:, 1:2, :HD].set(second_key)


def draw_request_owner(key, part):
    return layout(key)[0]


def draw_block_req(key, part):
    return layout(key)[1]


def draw_migrate(key, part):
    return layout(key)[2]


def draw_cache_pool(key, part):
    return cache_values(key).astype(jnp.bfloat16)


def draw_queries(key, part):
    query_key = jax.random.fold_in(key, 7)
    second = jax.random.fold_in(query_key, 1)
    extent = (REQ, HEADS * HD)
    values = jnp.clip(2.0 * jax.random.normal(second, extent, jnp.float32), -12.0, 12.0)
    return values.astype(jnp.bfloat16)


def levels(rng, shape, cuts, low, top_value):
    level = 1.0
    for axis_at, parts in cuts:
        heights = jax.random.uniform(jax.random.fold_in(jax.random.fold_in(rng, 6), axis_at), (parts,), jnp.float32, low / len(cuts), top_value / len(cuts))
        level = level * jnp.repeat(jnp.exp(heights), shape[axis_at] // parts).reshape((-1,) + (1,) * (len(shape) - 1 - axis_at))
    return level


def centred(own_key, shape, deviation, most, shards=(), kind=jnp.bfloat16):
    gain = levels(own_key, shape, shards, -0.22, 0.18) if shards else 1.0
    drawn = jax.random.normal(own_key, shape, jnp.float32) * deviation * gain
    return jnp.minimum(jnp.maximum(drawn, -most), most).astype(kind)


def setup_inputs(seed: int = 0, part: int = 0) -> dict:
    seeds = jax.random.split(jax.random.key(seed), 12)
    own_keys = jax.random.split(jax.random.fold_in(seeds[11], part), 12)
    return {
        "queries": draw_queries(jax.random.fold_in(jax.random.fold_in(seeds[11], part), 71), part),
        "new_kv": centred(own_keys[1], (REQ, 2 * HD), 1.0, 6.0, ((0, 4),)),
        "cache_pool": draw_cache_pool(jax.random.fold_in(jax.random.fold_in(seeds[11], part), 71), part),
        "request_owner": draw_request_owner(jax.random.fold_in(jax.random.fold_in(seeds[11], part), 71), part),
        "block_req": draw_block_req(jax.random.fold_in(jax.random.fold_in(seeds[11], part), 71), part),
        "migrate": draw_migrate(jax.random.fold_in(jax.random.fold_in(seeds[11], part), 71), part),
        "residual_rows": centred(own_keys[6], (REQ, D), 1.0, 6.0, ((1, 4),)),
        "w_out": centred(seeds[7], (HEADS * HD, D), (HEADS * HD) ** -0.5, 0.046875, ((0, 4), (1, 4))),
        "w_gate": centred(seeds[8], (D, FF), D ** -0.5, 0.0625, ((0, 4), (1, 4))),
        "w_up": centred(seeds[9], (D, FF), D ** -0.5, 0.0625, ((0, 4), (1, 4))),
        "w_down": centred(seeds[10], (FF, D), FF ** -0.5, 0.046875, ((0, 4), (1, 4))),
    }


def request_slots(request_owner):
    owner_grid = request_owner.reshape(N_ATTN, REQ_DEV)
    order = jnp.arange(REQ_DEV, dtype=jnp.int32)
    earlier = order[None, :] < order[:, None]
    same = owner_grid[:, :, None] == owner_grid[:, None, :]
    order_rank = jnp.sum(jnp.logical_and(same, earlier[None]), axis=2).astype(jnp.int32)
    within = (jnp.arange(N_ATTN, dtype=jnp.int32)[:, None] * CAP + order_rank).reshape(-1)
    return within.astype(jnp.int32)


def block_terms(blocks, query_rows):
    queries3 = query_rows.reshape(query_rows.shape[0], HEADS, HD).astype(jnp.float32)
    key_part = blocks[:, :, :HD].astype(jnp.float32)
    value_part = blocks[:, :, HD:].astype(jnp.float32)
    scores = jnp.einsum("ehd,etd->eht", queries3, key_part, precision=lax.Precision.HIGHEST) * (HD ** -0.5)
    block_top = jnp.max(scores, axis=2)
    weight = jnp.exp(scores - block_top[:, :, None]).astype(jnp.bfloat16)
    block_total = jnp.sum(weight.astype(jnp.float32), axis=2)
    summed = jnp.einsum("eht,etd->ehd", weight.astype(jnp.float32), value_part, precision=lax.Precision.HIGHEST)
    return block_top, block_total, summed


def arrivals(cache_pool, migrate):
    incoming = jnp.transpose(migrate, (1, 0, 2)).reshape(N_ATTN, N_ATTN * MPAIR)
    usable = incoming < POOL
    position_in = jnp.cumsum(usable.astype(jnp.int32), axis=1) - 1
    source = jnp.arange(N_ATTN * MPAIR, dtype=jnp.int32) // MPAIR
    flat_index = source[None, :] * POOL + jnp.minimum(incoming, POOL - 1)
    lanes = jnp.arange(R_IN, dtype=jnp.int32)
    matches = jnp.logical_and(usable[:, None, :], position_in[:, None, :] == lanes[None, :, None])
    present = jnp.any(matches, axis=2)
    chosen = jnp.argmax(matches, axis=2).astype(jnp.int32)
    picked = jnp.take_along_axis(flat_index, chosen, axis=1).reshape(-1).astype(jnp.int32)
    blocks = cache_pool[picked]
    empty = jnp.zeros_like(blocks)
    return jnp.where(present.reshape(-1)[:, None, None], blocks, empty)


def reference(queries, new_kv, cache_pool, request_owner, block_req, migrate, residual_rows, w_out, w_gate, w_up, w_down):
    within = request_slots(request_owner)
    slot_global = (request_owner * SLOTS + within).astype(jnp.int32)
    flat_req = block_req.reshape(-1)
    usable = flat_req < REQ
    picked = jnp.minimum(flat_req, REQ - 1).astype(jnp.int32)
    block_top, block_total, summed = block_terms(cache_pool, queries[picked])
    queries3 = queries.reshape(REQ, HEADS, HD).astype(jnp.float32)
    own_score = jnp.einsum("rhd,rd->rh", queries3, new_kv[:, :HD].astype(jnp.float32), precision=lax.Precision.HIGHEST) * (HD ** -0.5)
    own_value = new_kv[:, HD:].astype(jnp.float32)
    matches = jnp.logical_and(picked[None, :] == jnp.arange(REQ, dtype=jnp.int32)[:, None], usable[None, :])
    candidate = jnp.max(jnp.where(matches[:, :, None], block_top[None], -jnp.inf), axis=1)
    running_max = jnp.maximum(own_score, candidate)
    factor = jnp.where(matches[:, :, None], jnp.exp(block_top[None] - running_max[:, None]), 0.0)
    own_weight = jnp.exp(own_score - running_max)
    denominator = own_weight + jnp.sum(factor * block_total[None], axis=1)
    numerator = own_weight[:, :, None] * own_value[:, None, :] + jnp.einsum("rbh,bhd->rhd", factor, summed, precision=lax.Precision.HIGHEST)
    result = (numerator / denominator[:, :, None]).astype(jnp.bfloat16).reshape(REQ, HEADS * HD)
    attention = jnp.zeros((N_ATTN * SLOTS, HEADS * HD), jnp.bfloat16).at[slot_global].set(result)
    arrived = arrivals(cache_pool, migrate)
    projected = jnp.dot(result, w_out, preferred_element_type=jnp.float32)
    mixed = (residual_rows.astype(jnp.float32) + projected).astype(jnp.bfloat16)
    gate_sum = jnp.dot(mixed, w_gate, preferred_element_type=jnp.float32)
    up_sum = jnp.dot(mixed, w_up, preferred_element_type=jnp.float32)
    hidden = (jax.nn.silu(gate_sum) * up_sum).astype(jnp.bfloat16)
    ffn_out = (mixed.astype(jnp.float32) + jnp.dot(hidden, w_down, preferred_element_type=jnp.float32)).astype(jnp.bfloat16)
    return attention, arrived, ffn_out
```

```python
import functools

import jax
import jax.numpy as jnp
from jax import lax
from jax.experimental import pallas as pl
from jax.experimental.pallas import tpu as pltpu
from jax.sharding import PartitionSpec as P

CHUNKS = 2


def attention_kernel(
    slot_ref, live_ref, q_ref, kv_ref, pool_ref, out_ref, pages, sems, q3, top_ref, den_ref, num_ref
):
    page_count = pages.shape[0]
    heads, size = q3.shape[1], q3.shape[2]
    lanes = top_ref.shape[2]
    scale = size ** (-0.5)
    copies = [
        pltpu.make_async_copy(pool_ref.at[b], pages.at[b], sems.at[b]) for b in range(page_count)
    ]
    for copy in copies:
        copy.start()
    for h in range(heads):
        q3[:, h, :] = q_ref[:, h * size : (h + 1) * size].astype(jnp.float32)
    key = kv_ref[:, :size].astype(jnp.float32)
    own = jnp.sum(q3[...] * key[:, None, :], axis=2, keepdims=True) * scale
    top_ref[...] = jnp.broadcast_to(own, top_ref.shape)
    den_ref[...] = jnp.ones_like(den_ref)
    num_ref[...] = jnp.broadcast_to(kv_ref[:, size:].astype(jnp.float32)[:, None, :], num_ref.shape)
    terms = []
    for b in range(page_count):
        copies[b].wait()
        q = q3[slot_ref[b]].astype(jnp.bfloat16)
        scores = (
            lax.dot_general(
                q, pages[b, :, :size], (((1,), (1,)), ((), ())), preferred_element_type=jnp.float32
            )
            * scale
        )
        top = jnp.max(scores, axis=1, keepdims=True)
        weight = jnp.exp(scores - top).astype(jnp.bfloat16)
        total = jnp.sum(weight.astype(jnp.float32), axis=1, keepdims=True)
        summed = jnp.dot(weight, pages[b, :, size:], preferred_element_type=jnp.float32)
        top = jnp.where(b < live_ref[0], top, -jnp.inf)
        terms.append((top, total, summed))
    for b in range(page_count):
        top, total, summed = terms[b]
        slot = slot_ref[b]
        old = top_ref[slot]
        top = jnp.broadcast_to(top, old.shape)
        new = jnp.maximum(old, top)
        keep = jnp.exp(old - new)
        take = jnp.exp(top - new)
        top_ref[slot] = new
        den_ref[slot] = den_ref[slot] * keep + take * total
        num_ref[slot] = num_ref[slot] * keep[:, :1] + take[:, :1] * summed
    for h in range(heads):
        out_ref[:, h * size : (h + 1) * size] = (num_ref[:, h, :] / den_ref[:, h, :1]).astype(
            out_ref.dtype
        )


def attend(block_slot, live, slot_queries, slot_kv, cache_pool, heads, size):
    slots = slot_queries.shape[0]
    page_count = cache_pool.shape[0]
    smem = pl.BlockSpec(memory_space=pltpu.SMEM)
    vmem = pl.BlockSpec(memory_space=pltpu.VMEM)
    return pl.pallas_call(
        attention_kernel,
        out_shape=jax.ShapeDtypeStruct(slot_queries.shape, jnp.bfloat16),
        in_specs=[smem, smem, vmem, vmem, pl.BlockSpec(memory_space=pl.ANY)],
        out_specs=vmem,
        scratch_shapes=[
            pltpu.VMEM(cache_pool.shape, jnp.bfloat16),
            pltpu.SemaphoreType.DMA((page_count,)),
            pltpu.VMEM((slots, heads, size), jnp.float32),
            pltpu.VMEM((slots, heads, 128), jnp.float32),
            pltpu.VMEM((slots, heads, 128), jnp.float32),
            pltpu.VMEM((slots, heads, size), jnp.float32),
        ],
        compiler_params=pltpu.CompilerParams(vmem_limit_bytes=40 * 2**20),
        name="attention",
    )(block_slot, live, slot_queries, slot_kv, cache_pool)


def swap_perm(count, bit):
    return [(i, i ^ bit) for i in range(count)]


def block_swap(x, bit, on):
    order = jnp.stack([x[j ^ bit] for j in range(4)])
    return jnp.where(on, order, x)


def body(
    queries,
    new_kv,
    cache_pool,
    request_owner,
    block_req,
    migrate,
    residual_rows,
    w_out,
    w_gate,
    w_up,
    w_down,
):
    attn_count = lax.axis_size("attn")
    ffn_count = lax.axis_size("ffn")
    position = lax.axis_index("attn")
    ffn_position = lax.axis_index("ffn")
    req_dev = queries.shape[0]
    total_req = request_owner.shape[0]
    capacity = req_dev // 4
    slot_count = attn_count * capacity
    pool_count = cache_pool.shape[0]
    head_size = cache_pool.shape[2] // 2
    head_count = queries.shape[1] // head_size
    width = queries.shape[1]
    pair_room = migrate.shape[2]
    room_in = max(2, attn_count // 4) + 1
    paired = attn_count == 4

    owner_grid = request_owner.reshape(attn_count, req_dev)
    order = jnp.arange(req_dev, dtype=jnp.int32)
    earlier = order[None, :] < order[:, None]
    same = owner_grid[:, :, None] == owner_grid[:, None, :]
    order_rank = jnp.sum(jnp.logical_and(same, earlier[None]), axis=2)
    within = (jnp.arange(attn_count, dtype=jnp.int32)[:, None] * capacity + order_rank).reshape(-1)
    mine_owner = lax.dynamic_slice_in_dim(owner_grid, position, 1, 0)[0]
    mine_rank = lax.dynamic_slice_in_dim(order_rank, position, 1, 0)[0]
    target_slot = mine_owner * capacity + mine_rank
    picker = (jnp.arange(slot_count, dtype=jnp.int32)[:, None] == target_slot[None, :]).astype(
        jnp.bfloat16
    )
    send = jnp.dot(
        picker, jnp.concatenate([queries, new_kv], axis=1), preferred_element_type=jnp.float32
    ).astype(jnp.bfloat16)
    received = lax.all_to_all(
        send.reshape(attn_count, capacity, -1), "attn", split_axis=0, concat_axis=0, tiled=True
    ).reshape(slot_count, -1)
    my_req = lax.dynamic_slice_in_dim(block_req, position, 1, 0)[0]
    live_count = jnp.sum((my_req < total_req).astype(jnp.int32))
    block_slot = within[jnp.minimum(my_req, total_req - 1)]
    attention = attend(
        block_slot,
        live_count.reshape(1),
        received[:, :width],
        received[:, width:],
        cache_pool,
        head_count,
        head_size,
    )

    if paired:
        across = lax.ppermute(attention, "attn", swap_perm(4, 2))
        pair = jnp.concatenate([attention, across], axis=0)
        other = lax.ppermute(pair, "attn", swap_perm(4, 1))
        everyone = jnp.concatenate([pair, other], axis=0)
        distance = jnp.bitwise_xor(request_owner, position)
        place = distance // 2 + (distance % 2) * 2
    else:
        everyone = lax.all_gather(attention, "attn", axis=0, tiled=True)
        place = request_owner
    row_of = place * slot_count + within
    row_picker = (
        row_of[:, None] == jnp.arange(attn_count * slot_count, dtype=jnp.int32)[None, :]
    ).astype(jnp.bfloat16)
    ordered = jnp.dot(row_picker, everyone, preferred_element_type=jnp.float32).astype(jnp.bfloat16)

    row_share = total_req // ffn_count
    columns = w_out.shape[1]
    projected = jnp.dot(ordered, w_out, preferred_element_type=jnp.float32).astype(jnp.bfloat16)
    parts = lax.all_to_all(
        projected.reshape(ffn_count, row_share, columns), "ffn", split_axis=0, concat_axis=0, tiled=True
    )
    kept_residual = lax.dynamic_slice_in_dim(residual_rows, ffn_position * row_share, row_share, 0)
    kept = (
        kept_residual.astype(jnp.float32) + jnp.sum(parts.astype(jnp.float32), axis=0)
    ).astype(jnp.bfloat16)
    mixed = lax.all_to_all(
        jnp.broadcast_to(kept[None], (ffn_count, row_share, columns)),
        "ffn",
        split_axis=0,
        concat_axis=0,
        tiled=True,
    )

    my_moves = lax.dynamic_slice_in_dim(migrate, position, 1, 0)[0]
    sent_usable = (my_moves < pool_count).reshape(-1)
    sent_index = jnp.minimum(my_moves, pool_count - 1).reshape(-1)
    sent_blocks = jnp.take(cache_pool, sent_index, axis=0)
    sent_blocks = jnp.where(sent_usable[:, None, None], sent_blocks, jnp.zeros_like(sent_blocks))
    sent_blocks = sent_blocks.reshape(attn_count, pair_room, cache_pool.shape[1], 2 * head_size)
    sent_blocks, _ = lax.optimization_barrier((sent_blocks, attention))
    landed = lax.all_to_all(sent_blocks, "attn", split_axis=0, concat_axis=0, tiled=True)
    incoming = lax.dynamic_slice_in_dim(migrate, position, 1, 1)[:, 0, :].reshape(-1)
    came_usable = incoming < pool_count
    position_in = jnp.cumsum(came_usable.astype(jnp.int32)) - 1
    lanes = jnp.arange(room_in, dtype=jnp.int32)
    matches = jnp.logical_and(came_usable[None, :], position_in[None, :] == lanes[:, None])
    present = jnp.any(matches, axis=1)
    chosen = jnp.argmax(matches, axis=1)
    landed_flat = landed.reshape(attn_count * pair_room, landed.shape[2], landed.shape[3])
    arrived = jnp.take(landed_flat, chosen, axis=0)
    arrived = jnp.where(present[:, None, None], arrived, jnp.zeros_like(arrived))

    hidden_width = w_gate.shape[1]
    step = hidden_width // CHUNKS
    if paired:
        low, high = position % 2 == 1, position >= 2
        mixed4 = mixed.reshape(4, total_req // 4, columns)
        mixed4 = block_swap(block_swap(mixed4, 1, low), 2, high)
        rows = mixed4.reshape(total_req, columns)
        down = None
        for c in range(CHUNKS):
            cut = slice(c * step, (c + 1) * step)
            gate = jnp.dot(rows, w_gate[:, cut], preferred_element_type=jnp.float32)
            up = jnp.dot(rows, w_up[:, cut], preferred_element_type=jnp.float32)
            both = jnp.stack([gate, up]).reshape(2, 4, total_req // 4, step)
            sent = jnp.stack([both[:, 1], both[:, 3]]).astype(jnp.bfloat16)
            sib = lax.ppermute(sent, "attn", swap_perm(4, 1)).astype(jnp.float32)
            near = both[:, 0] + sib[0]
            far = (both[:, 2] + sib[1]).astype(jnp.bfloat16)
            sums = near + lax.ppermute(far, "attn", swap_perm(4, 2)).astype(jnp.float32)
            quarter = (jax.nn.silu(sums[0]) * sums[1]).astype(jnp.bfloat16)
            half = jnp.stack([quarter, lax.ppermute(quarter, "attn", swap_perm(4, 2))])
            other = lax.ppermute(half, "attn", swap_perm(4, 1))
            hidden = jnp.stack([half[0], other[0], half[1], other[1]]).reshape(total_req, step)
            term = jnp.dot(hidden, w_down[cut], preferred_element_type=jnp.float32)
            down = term if down is None else down + term
        down4 = down.astype(jnp.bfloat16).reshape(4, total_req // 4, columns)
        down4 = block_swap(block_swap(down4, 1, low), 2, high)
        down = down4.reshape(total_req, columns)
    else:
        rows = mixed.reshape(total_req, columns)
        gate = jnp.dot(rows, w_gate, preferred_element_type=jnp.float32)
        up = jnp.dot(rows, w_up, preferred_element_type=jnp.float32)
        gate, up = lax.psum_scatter((gate, up), "attn", scatter_dimension=0, tiled=True)
        quarter = (jax.nn.silu(gate) * up).astype(jnp.bfloat16)
        hidden = lax.all_gather(quarter, "attn", axis=0, tiled=True)
        down = jnp.dot(hidden, w_down, preferred_element_type=jnp.float32).astype(jnp.bfloat16)
    shares = lax.all_to_all(
        down.reshape(ffn_count, row_share, columns), "ffn", split_axis=0, concat_axis=0, tiled=True
    )
    ffn_out = (kept.astype(jnp.float32) + jnp.sum(shares.astype(jnp.float32), axis=0)).astype(
        jnp.bfloat16
    )
    return (attention, arrived, ffn_out)


def solution(mesh):
    placed = (
        P(("groups", "attn"), "ffn"),
        P(("groups", "attn"), None),
        P(("groups", "attn"), None, None),
        P("groups"),
        P("groups", None),
        P("groups", None, None),
        P("groups", "attn"),
        P("ffn", "attn"),
        P("attn", "ffn"),
        P("attn", "ffn"),
        P("ffn", "attn"),
    )
    return jax.shard_map(
        body,
        mesh=mesh,
        in_specs=placed,
        out_specs=(
            P(("groups", "attn"), "ffn"),
            P(("groups", "attn"), None, None),
            P(("groups", "ffn"), "attn"),
        ),
        check_vma=False,
    )
```

```python
import functools

import jax
import jax.numpy as jnp
from jax import lax
from jax.experimental import pallas as pl
from jax.experimental.pallas import tpu as pltpu
from jax.sharding import PartitionSpec as P

CHUNKS = 2


def attention_kernel(number_ref, *refs, distances):
    block_refs, refs = refs[: len(distances)], refs[len(distances) :]
    pool_ref, out_ref, twin_ref, *moved_refs, pages, move_sems, sems, q3, top_ref, den_ref, num_ref = refs
    page_count = pages.shape[0]
    place = number_ref[0]
    lanes = move_sems.shape[1]
    first = 1 + page_count + move_sems.shape[0] * lanes
    requests = number_ref.shape[0] - first
    heads, size = q3.shape[1], q3.shape[2]
    width = heads * size
    scale = size ** (-0.5)
    copies = [
        pltpu.make_async_copy(pool_ref.at[b], pages.at[b], sems.at[b]) for b in range(page_count)
    ]
    for copy in copies:
        copy.start()
    moves = []
    for d, moved_ref in enumerate(moved_refs):
        for m in range(moved_ref.shape[0]):
            page = number_ref[1 + page_count + jnp.bitwise_xor(place, d) * lanes + m]
            page = jnp.minimum(page, page_count - 1)
            moves.append(
                pltpu.make_async_copy(pool_ref.at[page], moved_ref.at[m], move_sems.at[d, m])
            )
    for move in moves:
        move.start()
    for i, block_ref in enumerate(block_refs):
        rows = block_ref.shape[0]
        at = pl.ds(jnp.bitwise_xor(place, distances[i]) * rows if len(distances) > 1 else 0, rows)
        for h in range(heads):
            q3[at, h, :] = block_ref[:, h * size : (h + 1) * size].astype(jnp.float32)
        key = block_ref[:, width : width + size].astype(jnp.float32)
        value = block_ref[:, width + size :].astype(jnp.float32)
        own = jnp.sum(q3[at] * key[:, None, :], axis=2, keepdims=True) * scale
        top_ref[at] = jnp.broadcast_to(own, (rows, heads, top_ref.shape[2]))
        num_ref[at] = jnp.broadcast_to(value[:, None, :], (rows, heads, size))
    den_ref[...] = jnp.ones_like(den_ref)
    terms = []
    slots = []
    for b in range(page_count):
        request = number_ref[1 + b]
        slots.append(number_ref[first + jnp.minimum(request, requests - 1)])
        copies[b].wait()
        q = q3[slots[b]].astype(jnp.bfloat16)
        scores = (
            lax.dot_general(
                q, pages[b, :, :size], (((1,), (1,)), ((), ())), preferred_element_type=jnp.float32
            )
            * scale
        )
        top = jnp.max(scores, axis=1, keepdims=True)
        weight = jnp.exp(scores - top).astype(jnp.bfloat16)
        total = jnp.sum(weight.astype(jnp.float32), axis=1, keepdims=True)
        summed = jnp.dot(weight, pages[b, :, size:], preferred_element_type=jnp.float32)
        top = jnp.where(request < requests, top, -jnp.inf)
        terms.append((top, total, summed))
    for b in range(page_count):
        top, total, summed = terms[b]
        slot = slots[b]
        old = top_ref[slot]
        top = jnp.broadcast_to(top, old.shape)
        new = jnp.maximum(old, top)
        keep = jnp.exp(old - new)
        take = jnp.exp(top - new)
        top_ref[slot] = new
        den_ref[slot] = den_ref[slot] * keep + take * total
        num_ref[slot] = num_ref[slot] * keep[:, :1] + take[:, :1] * summed
    for h in range(heads):
        cut = slice(h * size, (h + 1) * size)
        result = (num_ref[:, h, :] / den_ref[:, h, :1]).astype(out_ref.dtype)
        out_ref[:, cut] = result
        twin_ref[:, cut] = result
    for move in moves:
        move.wait()


def in_hbm(x):
    return pltpu.with_memory_space_constraint(x, pltpu.HBM)


def attend(numbers, room, received, distances, cache_pool, slots, heads, size):
    page_count = cache_pool.shape[0]
    moved = jax.ShapeDtypeStruct((room[1],) + cache_pool.shape[1:], cache_pool.dtype)
    moved = [moved] * (len(distances) if len(distances) > 1 else 0)
    smem = pl.BlockSpec(memory_space=pltpu.SMEM)
    vmem = pl.BlockSpec(memory_space=pltpu.VMEM)
    return pl.pallas_call(
        functools.partial(attention_kernel, distances=distances),
        out_shape=[jax.ShapeDtypeStruct((slots, heads * size), jnp.bfloat16)] * 2 + moved,
        in_specs=[smem] + [vmem] * len(received) + [pl.BlockSpec(memory_space=pl.ANY)],
        out_specs=[vmem, vmem] + [pl.BlockSpec(memory_space=pl.ANY)] * len(moved),
        scratch_shapes=[
            pltpu.VMEM(cache_pool.shape, jnp.bfloat16),
            pltpu.SemaphoreType.DMA(room),
            pltpu.SemaphoreType.DMA((page_count,)),
            pltpu.VMEM((slots, heads, size), jnp.float32),
            pltpu.VMEM((slots, heads, 128), jnp.float32),
            pltpu.VMEM((slots, heads, 128), jnp.float32),
            pltpu.VMEM((slots, heads, size), jnp.float32),
        ],
        compiler_params=pltpu.CompilerParams(vmem_limit_bytes=24 * 2**20),
        name="attention",
    )(numbers, *received, in_hbm(cache_pool))


def swap_perm(count, bit):
    return [(i, i ^ bit) for i in range(count)]


def tie(x, *others):
    return lax.optimization_barrier((x, others))[0]


def fold_first(sent, far, axis):
    came = lax.ppermute(sent, axis, swap_perm(4, 1))
    return came[0], (far + came[1].astype(jnp.float32)).astype(jnp.bfloat16)


def fold_last(leaving, own, axis):
    far = lax.ppermute(leaving, axis, swap_perm(4, 2))
    total = own[0].astype(jnp.float32)
    for part in own[1:]:
        total = total + part.astype(jnp.float32)
    return lax.optimization_barrier(total) + far.astype(jnp.float32)


def spread(x, axis):
    half = jnp.stack([x, lax.ppermute(x, axis, swap_perm(4, 2))])
    other = lax.ppermute(half, axis, swap_perm(4, 1))
    return jnp.stack([half[0], other[0], half[1], other[1]])


def split_store(block, columns, near_ref, far_ref, sent_ref):
    share = near_ref.shape[0]
    near_ref[:, columns] = block[:share].astype(near_ref.dtype)
    sent_ref[0, :, columns] = block[share : 2 * share].astype(sent_ref.dtype)
    far_ref[:, columns] = block[2 * share : 3 * share].astype(far_ref.dtype)
    sent_ref[1, :, columns] = block[3 * share :].astype(sent_ref.dtype)


def project_kernel(picker_ref, *refs):
    *piece_refs, w_ref, near_ref, far_ref, sent_ref, tiles, acc_ref, sems = refs
    count, depth = tiles.shape[0], tiles.shape[1]
    copies = [
        pltpu.make_async_copy(w_ref.at[pl.ds(i * depth, depth)], tiles.at[i], sems.at[i])
        for i in range(count)
    ]
    for copy in copies:
        copy.start()
    picker = picker_ref[...]
    for i in range(count):
        cut = slice(i * depth, (i + 1) * depth)
        rows = jnp.concatenate([piece_ref[:, cut] for piece_ref in piece_refs], axis=0)
        x = jnp.dot(picker, rows, preferred_element_type=jnp.float32).astype(jnp.bfloat16)
        copies[i].wait()
        for n in range(0, acc_ref.shape[1], 256):
            to = slice(n, n + 256)
            block = jnp.dot(x, tiles[i, :, to], preferred_element_type=jnp.float32)
            if i > 0:
                block += acc_ref[:, to]
            if i < count - 1:
                acc_ref[:, to] = block
            else:
                split_store(block, to, near_ref, far_ref, sent_ref)


def split_shapes(share, columns):
    return [
        jax.ShapeDtypeStruct((share, columns), jnp.float32),
        jax.ShapeDtypeStruct((share, columns), jnp.float32),
        jax.ShapeDtypeStruct((2, share, columns), jnp.bfloat16),
    ]


def project(picker, pieces, w):
    vmem = pl.BlockSpec(memory_space=pltpu.VMEM)
    depth, columns = w.shape
    tile = 512
    return pl.pallas_call(
        project_kernel,
        out_shape=split_shapes(picker.shape[0] // 4, columns),
        in_specs=[vmem] * (1 + len(pieces)) + [pl.BlockSpec(memory_space=pl.ANY)],
        out_specs=[vmem] * 3,
        scratch_shapes=[
            pltpu.VMEM((depth // tile, tile, columns), w.dtype),
            pltpu.VMEM((picker.shape[0], columns), jnp.float32),
            pltpu.SemaphoreType.DMA((depth // tile,)),
        ],
        compiler_params=pltpu.CompilerParams(vmem_limit_bytes=32 * 2**20),
        name="project",
    )(picker, *pieces, in_hbm(w))


def gate_kernel(x_ref, gate_ref, up_ref, near_ref, far_ref, sent_ref, tiles, sems, *, start):
    count, width = tiles.shape[0] // 2, tiles.shape[2]
    copies = []
    for i in range(2 * count):
        w_ref = gate_ref if i < count else up_ref
        at = pl.ds(start + (i % count) * width, width)
        copies.append(pltpu.make_async_copy(w_ref.at[:, at], tiles.at[i], sems.at[i]))
    for copy in copies:
        copy.start()
    x = x_ref[...]
    for i in range(2 * count):
        copies[i].wait()
        for n in range(0, width, 256):
            block = jnp.dot(x, tiles[i, :, n : n + 256], preferred_element_type=jnp.float32)
            at = i * width + n
            split_store(block, slice(at, at + 256), near_ref, far_ref, sent_ref)


def gate_and_up(x, w_gate, w_up, start, width):
    vmem = pl.BlockSpec(memory_space=pltpu.VMEM)
    hbm = pl.BlockSpec(memory_space=pl.ANY)
    tile = 768
    count = 2 * (width // tile)
    return pl.pallas_call(
        functools.partial(gate_kernel, start=start),
        out_shape=split_shapes(x.shape[0] // 4, 2 * width),
        in_specs=[vmem, hbm, hbm],
        out_specs=[vmem] * 3,
        scratch_shapes=[
            pltpu.VMEM((count, x.shape[1], tile), w_gate.dtype),
            pltpu.SemaphoreType.DMA((count,)),
        ],
        compiler_params=pltpu.CompilerParams(vmem_limit_bytes=32 * 2**20),
        name="gate_and_up",
    )(x, in_hbm(w_gate), in_hbm(w_up))


def in_vmem(w):
    return pltpu.with_memory_space_constraint(w, pltpu.VMEM)


def down_kernel(at_ref, *refs):
    *x_refs, w_ref, near_ref, far_ref, sent_ref, turned_ref = refs
    share = near_ref.shape[0]
    width = x_refs[0].shape[1]
    xs = [x_ref[...] for x_ref in x_refs]
    for n in range(0, w_ref.shape[1], 256):
        cut = slice(n, n + 256)
        block = sum(
            jnp.dot(x, w_ref[i * width : (i + 1) * width, cut], preferred_element_type=jnp.float32)
            for i, x in enumerate(xs)
        )
        for j in range(4):
            turned_ref[jnp.bitwise_xor(at_ref[0], j)] = block[j * share : (j + 1) * share]
        near_ref[:, cut] = turned_ref[0]
        sent_ref[0, :, cut] = turned_ref[1].astype(sent_ref.dtype)
        far_ref[:, cut] = turned_ref[2]
        sent_ref[1, :, cut] = turned_ref[3].astype(sent_ref.dtype)


def down_project(at, xs, w):
    share = xs[0].shape[0] // 4
    vmem = pl.BlockSpec(memory_space=pltpu.VMEM)
    return pl.pallas_call(
        down_kernel,
        out_shape=split_shapes(share, w.shape[1]),
        in_specs=[pl.BlockSpec(memory_space=pltpu.SMEM)] + [vmem] * (len(xs) + 1),
        out_specs=[vmem] * 3,
        scratch_shapes=[pltpu.VMEM((4, share, 256), jnp.float32)],
        compiler_params=pltpu.CompilerParams(vmem_limit_bytes=6 * 2**20),
        name="down_project",
    )(at.reshape(1), *xs, in_vmem(w))


def paired_rows(
    pieces, row_picker, residual, turn, position, pages, w_out, w_gate, w_up, w_down
):
    count = row_picker.shape[0]
    share = count // 4
    columns = w_out.shape[1]
    step = w_gate.shape[1] // CHUNKS
    mine = lax.dynamic_slice_in_dim(residual, turn * share, share, 0)
    pieces, mine, pages = lax.optimization_barrier((pieces, mine, pages))
    landed = list(pages)
    landed[2] = lax.ppermute(pages[2], "attn", swap_perm(4, 2))
    near, far, sent = project(row_picker, pieces, w_out)
    sent, landed[2], pages[1] = lax.optimization_barrier((sent, landed[2], pages[1]))
    landed[1] = lax.ppermute(pages[1], "attn", swap_perm(4, 1))
    came, leaving = fold_first(sent, far, "ffn")
    leaving, landed[1] = lax.optimization_barrier((leaving, landed[1]))
    kept = fold_last(leaving, (mine, near, came), "ffn").astype(jnp.bfloat16)
    mixed = spread(kept, "ffn")
    mixed, pages[3] = lax.optimization_barrier((mixed, pages[3]))
    landed[3] = lax.ppermute(pages[3], "attn", swap_perm(4, 3))
    rows = mixed.reshape(count, columns)

    stages = []
    for c in range(CHUNKS):
        near, far, sent = gate_and_up(rows, w_gate, w_up, c * step, step)
        if c == 0:
            sent, landed[3] = lax.optimization_barrier((sent, landed[3]))
        came, leaving = fold_first(sent, far, "attn")
        rows = tie(rows, leaving)
        stages.append((near, came, leaving))
    hiddens = []
    for c in range(CHUNKS):
        near, came, leaving = stages[c]
        sums = fold_last(leaving, (near, came), "attn")
        quarter = (jax.nn.silu(sums[:, :step]) * sums[:, step:]).astype(jnp.bfloat16)
        across = lax.ppermute(quarter, "attn", swap_perm(4, 2))
        if c + 1 < CHUNKS:
            across = tie(across, stages[c + 1][2])
        half = jnp.stack([quarter, across])
        other = lax.ppermute(half, "attn", swap_perm(4, 1))
        hidden = jnp.stack([half[0], other[0], half[1], other[1]]).reshape(count, step)
        hiddens.append(hidden)
    near, far, sent = down_project(position, hiddens, w_down)
    came, leaving = fold_first(sent, far, "ffn")
    kept = lax.dynamic_index_in_dim(mixed, position, 0, keepdims=False)
    total = fold_last(leaving, (kept, near, came), "ffn")
    return total.astype(jnp.bfloat16), landed


def settle(landed, incoming, pool_count, room_in, turn):
    came_usable = incoming < pool_count
    position_in = jnp.cumsum(came_usable.astype(jnp.int32)) - 1
    lanes = jnp.arange(room_in, dtype=jnp.int32)
    matches = jnp.logical_and(came_usable[None, :], position_in[None, :] == lanes[:, None])
    present = jnp.any(matches, axis=1)
    chosen = jnp.argmax(matches, axis=1)
    if turn is not None:
        pair_room = landed.shape[0] // 4
        chosen = jnp.bitwise_xor(chosen // pair_room, turn) * pair_room + chosen % pair_room
    arrived = jnp.take(landed, chosen, axis=0)
    return jnp.where(present[:, None, None], arrived, jnp.zeros_like(arrived))


def body(
    queries,
    new_kv,
    cache_pool,
    request_owner,
    block_req,
    migrate,
    residual_rows,
    w_out,
    w_gate,
    w_up,
    w_down,
):
    attn_count = lax.axis_size("attn")
    ffn_count = lax.axis_size("ffn")
    position = lax.axis_index("attn")
    ffn_position = lax.axis_index("ffn")
    req_dev = queries.shape[0]
    total_req = request_owner.shape[0]
    capacity = req_dev // 4
    slot_count = attn_count * capacity
    pool_count = cache_pool.shape[0]
    head_size = cache_pool.shape[2] // 2
    head_count = queries.shape[1] // head_size
    pair_room = migrate.shape[2]
    room_in = max(2, attn_count // 4) + 1
    paired = attn_count == 4 and ffn_count == 4

    owner_grid = request_owner.reshape(attn_count, req_dev)
    order = jnp.arange(req_dev, dtype=jnp.int32)
    earlier = order[None, :] < order[:, None]
    same = owner_grid[:, :, None] == owner_grid[:, None, :]
    order_rank = jnp.sum(jnp.logical_and(same, earlier[None]), axis=2)
    within = (jnp.arange(attn_count, dtype=jnp.int32)[:, None] * capacity + order_rank).reshape(-1)
    mine_owner = lax.dynamic_slice_in_dim(owner_grid, position, 1, 0)[0]
    mine_rank = lax.dynamic_slice_in_dim(order_rank, position, 1, 0)[0]
    target = jnp.bitwise_xor(mine_owner, position) if paired else mine_owner
    picker = (
        jnp.arange(slot_count, dtype=jnp.int32)[:, None] == (target * capacity + mine_rank)[None, :]
    ).astype(jnp.bfloat16)
    send = (
        jnp.dot(
            picker, jnp.concatenate([queries, new_kv], axis=1), preferred_element_type=jnp.float32
        )
        .astype(jnp.bfloat16)
        .reshape(attn_count, capacity, -1)
    )
    if paired:
        received = [send[0]] + [
            lax.ppermute(send[d], "attn", swap_perm(4, d)) for d in (2, 3, 1)
        ]
        distances = (0, 2, 3, 1)
    else:
        received = lax.all_to_all(send, "attn", split_axis=0, concat_axis=0, tiled=True)
        received = [received.reshape(slot_count, -1)]
        distances = (0,)
    my_moves = lax.dynamic_index_in_dim(migrate, position, 0, keepdims=False)
    numbers = jnp.concatenate(
        [
            position.astype(jnp.int32).reshape(1),
            lax.dynamic_index_in_dim(block_req, position, 0, keepdims=False),
            my_moves.reshape(-1),
            within,
        ]
    )
    attention, twin, *pages = attend(
        numbers,
        (attn_count, pair_room),
        received,
        distances,
        cache_pool,
        slot_count,
        head_count,
        head_size,
    )

    if paired:
        across = lax.ppermute(twin, "attn", swap_perm(4, 2))
        beside = lax.ppermute(twin, "attn", swap_perm(4, 1))
        corner = lax.ppermute(across, "attn", swap_perm(4, 1))
        everyone = [twin, across, beside, corner]
        distance = jnp.bitwise_xor(request_owner, position)
        place = distance // 2 + (distance % 2) * 2
    else:
        everyone = lax.all_gather(attention, "attn", axis=0, tiled=True)
        place = request_owner
    row_share = total_req // ffn_count
    row_of = (place * slot_count + within).reshape(ffn_count, row_share)
    if paired:
        turn = jnp.bitwise_xor(ffn_position, position)
        row_of = jnp.take(row_of, jnp.bitwise_xor(jnp.arange(4, dtype=jnp.int32), turn), axis=0)
    row_of = row_of.reshape(-1)
    row_picker = (
        row_of[:, None] == jnp.arange(attn_count * slot_count, dtype=jnp.int32)[None, :]
    ).astype(jnp.bfloat16)

    incoming = lax.dynamic_slice_in_dim(migrate, position, 1, 1)[:, 0, :].reshape(-1)
    if paired:
        ffn_out, landed = paired_rows(
            everyone, row_picker, residual_rows, turn, position, pages, w_out, w_gate, w_up, w_down
        )
        arrived = settle(jnp.concatenate(landed), incoming, pool_count, room_in, position)
        return (attention, arrived, ffn_out)

    sent_index = jnp.minimum(my_moves, pool_count - 1).reshape(-1)
    sent_blocks = jnp.take(cache_pool, sent_index, axis=0)
    sent_blocks = sent_blocks.reshape(attn_count, pair_room, cache_pool.shape[1], 2 * head_size)
    landed = lax.all_to_all(sent_blocks, "attn", split_axis=0, concat_axis=0, tiled=True)
    landed = landed.reshape(attn_count * pair_room, landed.shape[2], landed.shape[3])
    arrived = settle(landed, incoming, pool_count, room_in, None)

    ordered = jnp.dot(row_picker, everyone, preferred_element_type=jnp.float32).astype(jnp.bfloat16)
    columns = w_out.shape[1]
    projected = jnp.dot(ordered, w_out, preferred_element_type=jnp.float32).astype(jnp.bfloat16)
    parts = projected.reshape(ffn_count, row_share, columns)
    parts = lax.all_to_all(parts, "ffn", split_axis=0, concat_axis=0, tiled=True)
    mine = lax.dynamic_slice_in_dim(residual_rows, ffn_position * row_share, row_share, 0)
    kept = (mine.astype(jnp.float32) + jnp.sum(parts.astype(jnp.float32), axis=0)).astype(
        jnp.bfloat16
    )
    rows = lax.all_gather(kept, "ffn", axis=0, tiled=True)
    gate = jnp.dot(rows, w_gate, preferred_element_type=jnp.float32)
    up = jnp.dot(rows, w_up, preferred_element_type=jnp.float32)
    gate, up = lax.psum_scatter((gate, up), "attn", scatter_dimension=0, tiled=True)
    quarter = (jax.nn.silu(gate) * up).astype(jnp.bfloat16)
    hidden = lax.all_gather(quarter, "attn", axis=0, tiled=True)
    down = jnp.dot(hidden, w_down, preferred_element_type=jnp.float32).astype(jnp.bfloat16)
    shares = lax.all_to_all(
        down.reshape(ffn_count, row_share, columns), "ffn", split_axis=0, concat_axis=0, tiled=True
    )
    total = jnp.sum(shares.astype(jnp.float32), axis=0)
    ffn_out = (kept.astype(jnp.float32) + total).astype(jnp.bfloat16)
    return (attention, arrived, ffn_out)


def solution(mesh):
    placed = (
        P(("groups", "attn"), "ffn"),
        P(("groups", "attn"), None),
        P(("groups", "attn"), None, None),
        P("groups"),
        P("groups", None),
        P("groups", None, None),
        P("groups", "attn"),
        P("ffn", "attn"),
        P("attn", "ffn"),
        P("attn", "ffn"),
        P("ffn", "attn"),
    )
    return jax.shard_map(
        body,
        mesh=mesh,
        in_specs=placed,
        out_specs=(
            P(("groups", "attn"), "ffn"),
            P(("groups", "attn"), None, None),
            P(("groups", "ffn"), "attn"),
        ),
        check_vma=False,
    )
```

```python
import functools

import jax
import jax.numpy as jnp
from jax import lax
from jax.experimental import pallas as pl
from jax.experimental.pallas import tpu as pltpu
from jax.sharding import PartitionSpec as P

CHUNKS = 2
PARTS = 2


def attention_kernel(number_ref, *refs, distances):
    block_refs, refs = refs[: len(distances)], refs[len(distances) :]
    pool_ref, out_ref, twin_ref, *moved_refs, pages, move_sems, sems, q3, top_ref, den_ref, num_ref = refs
    page_count = pages.shape[0]
    place = number_ref[0]
    lanes = move_sems.shape[1]
    first = 1 + page_count + move_sems.shape[0] * lanes
    requests = number_ref.shape[0] - first
    heads, size = q3.shape[1], q3.shape[2]
    width = heads * size
    scale = size ** (-0.5)
    copies = [
        pltpu.make_async_copy(pool_ref.at[b], pages.at[b], sems.at[b]) for b in range(page_count)
    ]
    for copy in copies:
        copy.start()
    moves = []
    for d, moved_ref in enumerate(moved_refs):
        for m in range(moved_ref.shape[0]):
            page = number_ref[1 + page_count + jnp.bitwise_xor(place, d) * lanes + m]
            page = jnp.minimum(page, page_count - 1)
            moves.append(
                pltpu.make_async_copy(pool_ref.at[page], moved_ref.at[m], move_sems.at[d, m])
            )
    for move in moves:
        move.start()
    for i, block_ref in enumerate(block_refs):
        rows = block_ref.shape[0]
        at = pl.ds(jnp.bitwise_xor(place, distances[i]) * rows if len(distances) > 1 else 0, rows)
        for h in range(heads):
            q3[at, h, :] = block_ref[:, h * size : (h + 1) * size].astype(jnp.float32)
        key = block_ref[:, width : width + size].astype(jnp.float32)
        value = block_ref[:, width + size :].astype(jnp.float32)
        own = jnp.sum(q3[at] * key[:, None, :], axis=2, keepdims=True) * scale
        top_ref[at] = jnp.broadcast_to(own, (rows, heads, top_ref.shape[2]))
        num_ref[at] = jnp.broadcast_to(value[:, None, :], (rows, heads, size))
    den_ref[...] = jnp.ones_like(den_ref)
    terms = []
    slots = []
    for first_page in range(0, page_count, 7):
        group = range(first_page, min(first_page + 7, page_count))
        for b in group:
            copies[b].wait()
        live = []
        scores = []
        for b in group:
            request = number_ref[1 + b]
            slots.append(number_ref[first + jnp.minimum(request, requests - 1)])
            live.append(request < requests)
            q = q3[slots[b]].astype(jnp.bfloat16)
            scores.append(
                lax.dot_general(
                    q, pages[b, :, :size], (((1,), (1,)), ((), ())), preferred_element_type=jnp.float32
                )
                * scale
            )
        tops = [jnp.max(score, axis=1, keepdims=True) for score in scores]
        weights = [jnp.exp(score - top).astype(jnp.bfloat16) for score, top in zip(scores, tops)]
        for b, alive, top, weight in zip(group, live, tops, weights):
            total = jnp.sum(weight.astype(jnp.float32), axis=1, keepdims=True)
            summed = jnp.dot(weight, pages[b, :, size:], preferred_element_type=jnp.float32)
            terms.append((jnp.where(alive, top, -jnp.inf), total, summed))
    for b in range(page_count):
        top, total, summed = terms[b]
        slot = slots[b]
        old = top_ref[slot]
        top = jnp.broadcast_to(top, old.shape)
        new = jnp.maximum(old, top)
        keep = jnp.exp(old - new)
        take = jnp.exp(top - new)
        top_ref[slot] = new
        den_ref[slot] = den_ref[slot] * keep + take * total
        num_ref[slot] = num_ref[slot] * keep[:, :1] + take[:, :1] * summed
    for h in range(heads):
        cut = slice(h * size, (h + 1) * size)
        result = (num_ref[:, h, :] / den_ref[:, h, :1]).astype(out_ref.dtype)
        out_ref[:, cut] = result
        twin_ref[:, cut] = result
    for move in moves:
        move.wait()


def in_hbm(x):
    return pltpu.with_memory_space_constraint(x, pltpu.HBM)


def attend(numbers, room, received, distances, cache_pool, slots, heads, size):
    page_count = cache_pool.shape[0]
    moved = jax.ShapeDtypeStruct((room[1],) + cache_pool.shape[1:], cache_pool.dtype)
    moved = [moved] * (len(distances) if len(distances) > 1 else 0)
    smem = pl.BlockSpec(memory_space=pltpu.SMEM)
    vmem = pl.BlockSpec(memory_space=pltpu.VMEM)
    return pl.pallas_call(
        functools.partial(attention_kernel, distances=distances),
        out_shape=[jax.ShapeDtypeStruct((slots, heads * size), jnp.bfloat16)] * 2 + moved,
        in_specs=[smem] + [vmem] * len(received) + [pl.BlockSpec(memory_space=pl.ANY)],
        out_specs=[vmem, vmem] + [pl.BlockSpec(memory_space=pl.ANY)] * len(moved),
        scratch_shapes=[
            pltpu.VMEM(cache_pool.shape, jnp.bfloat16),
            pltpu.SemaphoreType.DMA(room),
            pltpu.SemaphoreType.DMA((page_count,)),
            pltpu.VMEM((slots, heads, size), jnp.float32),
            pltpu.VMEM((slots, heads, 128), jnp.float32),
            pltpu.VMEM((slots, heads, 128), jnp.float32),
            pltpu.VMEM((slots, heads, size), jnp.float32),
        ],
        compiler_params=pltpu.CompilerParams(vmem_limit_bytes=24 * 2**20),
        name="attention",
    )(numbers, *received, in_hbm(cache_pool))


def swap_perm(count, bit):
    return [(i, i ^ bit) for i in range(count)]


def tie(x, *others):
    return lax.optimization_barrier((x, others))[0]


def fold_first(sent, far, axis):
    came = lax.ppermute(sent, axis, swap_perm(4, 1))
    return came[0], (far + came[1].astype(jnp.float32)).astype(jnp.bfloat16)


def fold_last(leaving, own, axis):
    far = lax.ppermute(leaving, axis, swap_perm(4, 2))
    total = own[0].astype(jnp.float32)
    for part in own[1:]:
        total = total + part.astype(jnp.float32)
    return lax.optimization_barrier(total) + far.astype(jnp.float32)


def spread(x, axis):
    half = jnp.stack([x, lax.ppermute(x, axis, swap_perm(4, 2))])
    other = lax.ppermute(half, axis, swap_perm(4, 1))
    return jnp.stack([half[0], other[0], half[1], other[1]])


def split_store(block, columns, near_ref, far_ref, sent_ref):
    share = near_ref.shape[0]
    near_ref[:, columns] = block[:share].astype(near_ref.dtype)
    sent_ref[0, :, columns] = block[share : 2 * share].astype(sent_ref.dtype)
    far_ref[:, columns] = block[2 * share : 3 * share].astype(far_ref.dtype)
    sent_ref[1, :, columns] = block[3 * share :].astype(sent_ref.dtype)


def project_kernel(picker_ref, *refs):
    *piece_refs, w_ref, near_ref, far_ref, sent_ref, tiles, acc_ref, sems = refs
    count, depth = tiles.shape[0], tiles.shape[1]
    copies = [
        pltpu.make_async_copy(w_ref.at[pl.ds(i * depth, depth)], tiles.at[i], sems.at[i])
        for i in range(count)
    ]
    for copy in copies:
        copy.start()
    picker = picker_ref[...]
    for i in range(count):
        cut = slice(i * depth, (i + 1) * depth)
        rows = jnp.concatenate([piece_ref[:, cut] for piece_ref in piece_refs], axis=0)
        x = jnp.dot(picker, rows, preferred_element_type=jnp.float32).astype(jnp.bfloat16)
        copies[i].wait()
        for n in range(0, acc_ref.shape[1], 256):
            to = slice(n, n + 256)
            block = jnp.dot(x, tiles[i, :, to], preferred_element_type=jnp.float32)
            if i > 0:
                block += acc_ref[:, to]
            if i < count - 1:
                acc_ref[:, to] = block
            else:
                split_store(block, to, near_ref, far_ref, sent_ref)


def split_shapes(share, columns):
    return [
        jax.ShapeDtypeStruct((share, columns), jnp.float32),
        jax.ShapeDtypeStruct((share, columns), jnp.float32),
        jax.ShapeDtypeStruct((2, share, columns), jnp.bfloat16),
    ]


def project(picker, pieces, w):
    vmem = pl.BlockSpec(memory_space=pltpu.VMEM)
    depth, columns = w.shape
    tile = 512
    return pl.pallas_call(
        project_kernel,
        out_shape=split_shapes(picker.shape[0] // 4, columns),
        in_specs=[vmem] * (1 + len(pieces)) + [pl.BlockSpec(memory_space=pl.ANY)],
        out_specs=[vmem] * 3,
        scratch_shapes=[
            pltpu.VMEM((depth // tile, tile, columns), w.dtype),
            pltpu.VMEM((picker.shape[0], columns), jnp.float32),
            pltpu.SemaphoreType.DMA((depth // tile,)),
        ],
        compiler_params=pltpu.CompilerParams(vmem_limit_bytes=32 * 2**20),
        name="project",
    )(picker, *pieces, in_hbm(w))


def gate_kernel(x_ref, gate_ref, up_ref, near_ref, far_ref, sent_ref, tiles, sems, *, start):
    count, width = tiles.shape[0] // 2, tiles.shape[2]
    copies = []
    for i in range(2 * count):
        w_ref = gate_ref if i < count else up_ref
        at = pl.ds(start + (i % count) * width, width)
        copies.append(pltpu.make_async_copy(w_ref.at[:, at], tiles.at[i], sems.at[i]))
    for copy in copies:
        copy.start()
    x = x_ref[...]
    for i in range(2 * count):
        copies[i].wait()
        for n in range(0, width, 256):
            block = jnp.dot(x, tiles[i, :, n : n + 256], preferred_element_type=jnp.float32)
            at = i * width + n
            split_store(block, slice(at, at + 256), near_ref, far_ref, sent_ref)


def gate_and_up(x, w_gate, w_up, start, width):
    vmem = pl.BlockSpec(memory_space=pltpu.VMEM)
    hbm = pl.BlockSpec(memory_space=pl.ANY)
    tile = 768
    count = 2 * (width // tile)
    return pl.pallas_call(
        functools.partial(gate_kernel, start=start),
        out_shape=split_shapes(x.shape[0] // 4, 2 * width),
        in_specs=[vmem, hbm, hbm],
        out_specs=[vmem] * 3,
        scratch_shapes=[
            pltpu.VMEM((count, x.shape[1], tile), w_gate.dtype),
            pltpu.SemaphoreType.DMA((count,)),
        ],
        compiler_params=pltpu.CompilerParams(vmem_limit_bytes=32 * 2**20),
        name="gate_and_up",
    )(x, in_hbm(w_gate), in_hbm(w_up))


def in_vmem(w):
    return pltpu.with_memory_space_constraint(w, pltpu.VMEM)


def down_kernel(at_ref, *refs):
    refs, turned_ref = refs[:-1], refs[-1]
    refs, outs = refs[: -3 * PARTS], refs[-3 * PARTS :]
    *x_refs, w_ref = refs
    share, columns = outs[0].shape
    width = x_refs[0].shape[1]
    xs = [x_ref[...] for x_ref in x_refs]
    for p in range(PARTS):
        near_ref, far_ref, sent_ref = outs[3 * p : 3 * p + 3]
        for n in range(0, columns, 256):
            cut = slice(n, min(n + 256, columns))
            size = cut.stop - cut.start
            at = pl.ds(p * columns + n, size)
            block = sum(
                jnp.dot(x, w_ref[i * width : (i + 1) * width, at], preferred_element_type=jnp.float32)
                for i, x in enumerate(xs)
            )
            for j in range(4):
                turned_ref[jnp.bitwise_xor(at_ref[0], j), :, :size] = block[
                    j * share : (j + 1) * share
                ]
            near_ref[:, cut] = turned_ref[0, :, :size]
            sent_ref[0, :, cut] = turned_ref[1, :, :size].astype(sent_ref.dtype)
            far_ref[:, cut] = turned_ref[2, :, :size]
            sent_ref[1, :, cut] = turned_ref[3, :, :size].astype(sent_ref.dtype)


def down_project(at, xs, w):
    share = xs[0].shape[0] // 4
    vmem = pl.BlockSpec(memory_space=pltpu.VMEM)
    outs = pl.pallas_call(
        down_kernel,
        out_shape=split_shapes(share, w.shape[1] // PARTS) * PARTS,
        in_specs=[pl.BlockSpec(memory_space=pltpu.SMEM)] + [vmem] * (len(xs) + 1),
        out_specs=[vmem] * (3 * PARTS),
        scratch_shapes=[pltpu.VMEM((4, share, 256), jnp.float32)],
        compiler_params=pltpu.CompilerParams(vmem_limit_bytes=6 * 2**20),
        name="down_project",
    )(at.reshape(1), *xs, in_vmem(w))
    return [outs[3 * p : 3 * p + 3] for p in range(PARTS)]


def sum_first(sums):
    near, leaving = [], []
    for at_hand, far, sent in sums:
        came = lax.ppermute(sent, "ffn", swap_perm(4, 1))
        if leaving:
            came = tie(came, leaving[-1])
        near.append((at_hand, came[0]))
        leaving.append((far + came[1].astype(jnp.float32)).astype(jnp.bfloat16))
    return near, leaving


def sum_last(leaving, own, near):
    outs = []
    for p, last in enumerate(leaving):
        far = lax.ppermute(last, "ffn", swap_perm(4, 2))
        far = tie(far, outs[-1] if outs else leaving[-1])
        base = own[p].astype(jnp.float32) + near[p][0] + near[p][1].astype(jnp.float32)
        outs.append((lax.optimization_barrier(base) + far.astype(jnp.float32)).astype(jnp.bfloat16))
    return outs


def paired_rows(
    pieces, row_picker, residual, turn, position, pages, w_out, w_gate, w_up, w_down
):
    count = row_picker.shape[0]
    share = count // 4
    columns = w_out.shape[1]
    step = w_gate.shape[1] // CHUNKS
    mine = lax.dynamic_slice_in_dim(residual, turn * share, share, 0)
    pieces, mine, pages = lax.optimization_barrier((pieces, mine, pages))
    landed = list(pages)
    landed[2] = lax.ppermute(pages[2], "attn", swap_perm(4, 2))
    near, far, sent = project(row_picker, pieces, w_out)
    sent, landed[2], pages[1] = lax.optimization_barrier((sent, landed[2], pages[1]))
    landed[1] = lax.ppermute(pages[1], "attn", swap_perm(4, 1))
    came, leaving = fold_first(sent, far, "ffn")
    leaving, landed[1] = lax.optimization_barrier((leaving, landed[1]))
    kept = fold_last(leaving, (mine, near, came), "ffn").astype(jnp.bfloat16)
    mixed = spread(kept, "ffn")
    mixed, pages[3] = lax.optimization_barrier((mixed, pages[3]))
    landed[3] = lax.ppermute(pages[3], "attn", swap_perm(4, 3))
    rows = mixed.reshape(count, columns)

    stages = []
    for c in range(CHUNKS):
        near, far, sent = gate_and_up(rows, w_gate, w_up, c * step, step)
        if c == 0:
            sent, landed[3] = lax.optimization_barrier((sent, landed[3]))
        came, leaving = fold_first(sent, far, "attn")
        rows = tie(rows, leaving)
        stages.append((near, came, leaving))
    hiddens = []
    for c in range(CHUNKS):
        near, came, leaving = stages[c]
        sums = fold_last(leaving, (near, came), "attn")
        quarter = (jax.nn.silu(sums[:, :step]) * sums[:, step:]).astype(jnp.bfloat16)
        across = lax.ppermute(quarter, "attn", swap_perm(4, 2))
        if c + 1 < CHUNKS:
            across = tie(across, stages[c + 1][2])
        half = jnp.stack([quarter, across])
        other = lax.ppermute(half, "attn", swap_perm(4, 1))
        hidden = jnp.stack([half[0], other[0], half[1], other[1]]).reshape(count, step)
        hiddens.append(hidden)
    sums = down_project(position, hiddens, w_down)
    sums, landed = lax.optimization_barrier((sums, landed))
    near, leaving = sum_first(sums)
    kept = lax.dynamic_index_in_dim(mixed, position, 0, keepdims=False)
    part = columns // PARTS
    outs = sum_last(leaving, [kept[:, p * part : (p + 1) * part] for p in range(PARTS)], near)
    return jnp.concatenate(outs, axis=1), landed


def settle(landed, incoming, pool_count, room_in, turn):
    came_usable = incoming < pool_count
    position_in = jnp.cumsum(came_usable.astype(jnp.int32)) - 1
    lanes = jnp.arange(room_in, dtype=jnp.int32)
    matches = jnp.logical_and(came_usable[None, :], position_in[None, :] == lanes[:, None])
    present = jnp.any(matches, axis=1)
    chosen = jnp.argmax(matches, axis=1)
    if turn is not None:
        pair_room = landed.shape[0] // 4
        chosen = jnp.bitwise_xor(chosen // pair_room, turn) * pair_room + chosen % pair_room
    arrived = jnp.take(landed, chosen, axis=0)
    return jnp.where(present[:, None, None], arrived, jnp.zeros_like(arrived))


def body(
    queries,
    new_kv,
    cache_pool,
    request_owner,
    block_req,
    migrate,
    residual_rows,
    w_out,
    w_gate,
    w_up,
    w_down,
):
    attn_count = lax.axis_size("attn")
    ffn_count = lax.axis_size("ffn")
    position = lax.axis_index("attn")
    ffn_position = lax.axis_index("ffn")
    req_dev = queries.shape[0]
    total_req = request_owner.shape[0]
    capacity = req_dev // 4
    slot_count = attn_count * capacity
    pool_count = cache_pool.shape[0]
    head_size = cache_pool.shape[2] // 2
    head_count = queries.shape[1] // head_size
    pair_room = migrate.shape[2]
    room_in = max(2, attn_count // 4) + 1
    paired = attn_count == 4 and ffn_count == 4

    owner_grid = request_owner.reshape(attn_count, req_dev)
    order = jnp.arange(req_dev, dtype=jnp.int32)
    earlier = order[None, :] < order[:, None]
    same = owner_grid[:, :, None] == owner_grid[:, None, :]
    order_rank = jnp.sum(jnp.logical_and(same, earlier[None]), axis=2)
    within = (jnp.arange(attn_count, dtype=jnp.int32)[:, None] * capacity + order_rank).reshape(-1)
    mine_owner = lax.dynamic_slice_in_dim(owner_grid, position, 1, 0)[0]
    mine_rank = lax.dynamic_slice_in_dim(order_rank, position, 1, 0)[0]
    target = jnp.bitwise_xor(mine_owner, position) if paired else mine_owner
    picker = (
        jnp.arange(slot_count, dtype=jnp.int32)[:, None] == (target * capacity + mine_rank)[None, :]
    ).astype(jnp.bfloat16)
    send = (
        jnp.dot(
            picker, jnp.concatenate([queries, new_kv], axis=1), preferred_element_type=jnp.float32
        )
        .astype(jnp.bfloat16)
        .reshape(attn_count, capacity, -1)
    )
    if paired:
        received = [send[0]] + [
            lax.ppermute(send[d], "attn", swap_perm(4, d)) for d in (2, 3, 1)
        ]
        distances = (0, 2, 3, 1)
    else:
        received = lax.all_to_all(send, "attn", split_axis=0, concat_axis=0, tiled=True)
        received = [received.reshape(slot_count, -1)]
        distances = (0,)
    my_moves = lax.dynamic_index_in_dim(migrate, position, 0, keepdims=False)
    numbers = jnp.concatenate(
        [
            position.astype(jnp.int32).reshape(1),
            lax.dynamic_index_in_dim(block_req, position, 0, keepdims=False),
            my_moves.reshape(-1),
            within,
        ]
    )
    attention, twin, *pages = attend(
        numbers,
        (attn_count, pair_room),
        received,
        distances,
        cache_pool,
        slot_count,
        head_count,
        head_size,
    )

    if paired:
        across = lax.ppermute(twin, "attn", swap_perm(4, 2))
        beside = lax.ppermute(twin, "attn", swap_perm(4, 1))
        corner = lax.ppermute(across, "attn", swap_perm(4, 1))
        everyone = [twin, across, beside, corner]
        distance = jnp.bitwise_xor(request_owner, position)
        place = distance // 2 + (distance % 2) * 2
    else:
        everyone = lax.all_gather(attention, "attn", axis=0, tiled=True)
        place = request_owner
    row_share = total_req // ffn_count
    row_of = (place * slot_count + within).reshape(ffn_count, row_share)
    if paired:
        turn = jnp.bitwise_xor(ffn_position, position)
        row_of = jnp.take(row_of, jnp.bitwise_xor(jnp.arange(4, dtype=jnp.int32), turn), axis=0)
    row_of = row_of.reshape(-1)
    row_picker = (
        row_of[:, None] == jnp.arange(attn_count * slot_count, dtype=jnp.int32)[None, :]
    ).astype(jnp.bfloat16)

    incoming = lax.dynamic_slice_in_dim(migrate, position, 1, 1)[:, 0, :].reshape(-1)
    if paired:
        ffn_out, landed = paired_rows(
            everyone, row_picker, residual_rows, turn, position, pages, w_out, w_gate, w_up, w_down
        )
        arrived = settle(jnp.concatenate(landed), incoming, pool_count, room_in, position)
        return (attention, arrived, ffn_out)

    sent_index = jnp.minimum(my_moves, pool_count - 1).reshape(-1)
    sent_blocks = jnp.take(cache_pool, sent_index, axis=0)
    sent_blocks = sent_blocks.reshape(attn_count, pair_room, cache_pool.shape[1], 2 * head_size)
    landed = lax.all_to_all(sent_blocks, "attn", split_axis=0, concat_axis=0, tiled=True)
    landed = landed.reshape(attn_count * pair_room, landed.shape[2], landed.shape[3])
    arrived = settle(landed, incoming, pool_count, room_in, None)

    ordered = jnp.dot(row_picker, everyone, preferred_element_type=jnp.float32).astype(jnp.bfloat16)
    columns = w_out.shape[1]
    projected = jnp.dot(ordered, w_out, preferred_element_type=jnp.float32).astype(jnp.bfloat16)
    parts = projected.reshape(ffn_count, row_share, columns)
    parts = lax.all_to_all(parts, "ffn", split_axis=0, concat_axis=0, tiled=True)
    mine = lax.dynamic_slice_in_dim(residual_rows, ffn_position * row_share, row_share, 0)
    kept = (mine.astype(jnp.float32) + jnp.sum(parts.astype(jnp.float32), axis=0)).astype(
        jnp.bfloat16
    )
    rows = lax.all_gather(kept, "ffn", axis=0, tiled=True)
    gate = jnp.dot(rows, w_gate, preferred_element_type=jnp.float32)
    up = jnp.dot(rows, w_up, preferred_element_type=jnp.float32)
    gate, up = lax.psum_scatter((gate, up), "attn", scatter_dimension=0, tiled=True)
    quarter = (jax.nn.silu(gate) * up).astype(jnp.bfloat16)
    hidden = lax.all_gather(quarter, "attn", axis=0, tiled=True)
    down = jnp.dot(hidden, w_down, preferred_element_type=jnp.float32).astype(jnp.bfloat16)
    shares = lax.all_to_all(
        down.reshape(ffn_count, row_share, columns), "ffn", split_axis=0, concat_axis=0, tiled=True
    )
    total = jnp.sum(shares.astype(jnp.float32), axis=0)
    ffn_out = (kept.astype(jnp.float32) + total).astype(jnp.bfloat16)
    return (attention, arrived, ffn_out)


def solution(mesh):
    placed = (
        P(("groups", "attn"), "ffn"),
        P(("groups", "attn"), None),
        P(("groups", "attn"), None, None),
        P("groups"),
        P("groups", None),
        P("groups", None, None),
        P("groups", "attn"),
        P("ffn", "attn"),
        P("attn", "ffn"),
        P("attn", "ffn"),
        P("ffn", "attn"),
    )
    return jax.shard_map(
        body,
        mesh=mesh,
        in_specs=placed,
        out_specs=(
            P(("groups", "attn"), "ffn"),
            P(("groups", "attn"), None, None),
            P(("groups", "ffn"), "attn"),
        ),
        check_vma=False,
    )
```

```python
import functools

import jax
import jax.numpy as jnp
from jax import lax
from jax.experimental import pallas as pl
from jax.experimental.pallas import tpu as pltpu
from jax.sharding import PartitionSpec as P

CHUNKS = 2
PARTS = 1


def attention_kernel(number_ref, *refs, distances):
    block_refs, refs = refs[: len(distances)], refs[len(distances) :]
    pool_ref, out_ref, twin_ref, *moved_refs, pages, move_sems, sems, q3, top_ref, den_ref, num_ref = refs
    page_count = pages.shape[0]
    place = number_ref[0]
    lanes = move_sems.shape[1]
    first = 1 + page_count + move_sems.shape[0] * lanes
    requests = number_ref.shape[0] - first
    heads, size = q3.shape[1], q3.shape[2]
    width = heads * size
    scale = size ** (-0.5)
    copies = [
        pltpu.make_async_copy(pool_ref.at[b], pages.at[b], sems.at[b]) for b in range(page_count)
    ]
    for copy in copies:
        copy.start()
    moves = []
    for d, moved_ref in enumerate(moved_refs):
        for m in range(moved_ref.shape[0]):
            page = number_ref[1 + page_count + jnp.bitwise_xor(place, d) * lanes + m]
            page = jnp.minimum(page, page_count - 1)
            moves.append(
                pltpu.make_async_copy(pool_ref.at[page], moved_ref.at[m], move_sems.at[d, m])
            )
    for move in moves:
        move.start()
    for i, block_ref in enumerate(block_refs):
        rows = block_ref.shape[0]
        at = pl.ds(jnp.bitwise_xor(place, distances[i]) * rows if len(distances) > 1 else 0, rows)
        for h in range(heads):
            q3[at, h, :] = block_ref[:, h * size : (h + 1) * size].astype(jnp.float32)
        key = block_ref[:, width : width + size].astype(jnp.float32)
        value = block_ref[:, width + size :].astype(jnp.float32)
        own = jnp.sum(q3[at] * key[:, None, :], axis=2, keepdims=True) * scale
        top_ref[at] = jnp.broadcast_to(own, (rows, heads, top_ref.shape[2]))
        num_ref[at] = jnp.broadcast_to(value[:, None, :], (rows, heads, size))
    den_ref[...] = jnp.ones_like(den_ref)
    terms = []
    slots = []
    for first_page in range(0, page_count, 7):
        group = range(first_page, min(first_page + 7, page_count))
        for b in group:
            copies[b].wait()
        live = []
        scores = []
        for b in group:
            request = number_ref[1 + b]
            slots.append(number_ref[first + jnp.minimum(request, requests - 1)])
            live.append(request < requests)
            q = q3[slots[b]].astype(jnp.bfloat16)
            scores.append(
                lax.dot_general(
                    q, pages[b, :, :size], (((1,), (1,)), ((), ())), preferred_element_type=jnp.float32
                )
                * scale
            )
        tops = [jnp.max(score, axis=1, keepdims=True) for score in scores]
        weights = [jnp.exp(score - top).astype(jnp.bfloat16) for score, top in zip(scores, tops)]
        for b, alive, top, weight in zip(group, live, tops, weights):
            total = jnp.sum(weight.astype(jnp.float32), axis=1, keepdims=True)
            summed = jnp.dot(weight, pages[b, :, size:], preferred_element_type=jnp.float32)
            terms.append((jnp.where(alive, top, -jnp.inf), total, summed))
    for b in range(page_count):
        top, total, summed = terms[b]
        slot = slots[b]
        old = top_ref[slot]
        top = jnp.broadcast_to(top, old.shape)
        new = jnp.maximum(old, top)
        keep = jnp.exp(old - new)
        take = jnp.exp(top - new)
        top_ref[slot] = new
        den_ref[slot] = den_ref[slot] * keep + take * total
        num_ref[slot] = num_ref[slot] * keep[:, :1] + take[:, :1] * summed
    for h in range(heads):
        cut = slice(h * size, (h + 1) * size)
        result = (num_ref[:, h, :] / den_ref[:, h, :1]).astype(out_ref.dtype)
        out_ref[:, cut] = result
        twin_ref[:, cut] = result
    for move in moves:
        move.wait()


def in_hbm(x):
    return pltpu.with_memory_space_constraint(x, pltpu.HBM)


def attend(numbers, room, received, distances, cache_pool, slots, heads, size):
    page_count = cache_pool.shape[0]
    moved = jax.ShapeDtypeStruct((room[1],) + cache_pool.shape[1:], cache_pool.dtype)
    moved = [moved] * (len(distances) if len(distances) > 1 else 0)
    smem = pl.BlockSpec(memory_space=pltpu.SMEM)
    vmem = pl.BlockSpec(memory_space=pltpu.VMEM)
    return pl.pallas_call(
        functools.partial(attention_kernel, distances=distances),
        out_shape=[jax.ShapeDtypeStruct((slots, heads * size), jnp.bfloat16)] * 2 + moved,
        in_specs=[smem] + [vmem] * len(received) + [pl.BlockSpec(memory_space=pl.ANY)],
        out_specs=[vmem, vmem] + [pl.BlockSpec(memory_space=pl.ANY)] * len(moved),
        scratch_shapes=[
            pltpu.VMEM(cache_pool.shape, jnp.bfloat16),
            pltpu.SemaphoreType.DMA(room),
            pltpu.SemaphoreType.DMA((page_count,)),
            pltpu.VMEM((slots, heads, size), jnp.float32),
            pltpu.VMEM((slots, heads, 128), jnp.float32),
            pltpu.VMEM((slots, heads, 128), jnp.float32),
            pltpu.VMEM((slots, heads, size), jnp.float32),
        ],
        compiler_params=pltpu.CompilerParams(vmem_limit_bytes=24 * 2**20),
        name="attention",
    )(numbers, *received, in_hbm(cache_pool))


def swap_perm(count, bit):
    return [(i, i ^ bit) for i in range(count)]


def tie(x, *others):
    return lax.optimization_barrier((x, others))[0]


def fold_first(sent, far, axis):
    came = lax.ppermute(sent, axis, swap_perm(4, 1))
    return came[0], (far + came[1].astype(jnp.float32)).astype(jnp.bfloat16)


def fold_last(leaving, own, axis):
    far = lax.ppermute(leaving, axis, swap_perm(4, 2))
    total = own[0].astype(jnp.float32)
    for part in own[1:]:
        total = total + part.astype(jnp.float32)
    return lax.optimization_barrier(total) + far.astype(jnp.float32)


def spread(x, axis):
    half = jnp.stack([x, lax.ppermute(x, axis, swap_perm(4, 2))])
    other = lax.ppermute(half, axis, swap_perm(4, 1))
    return jnp.stack([half[0], other[0], half[1], other[1]])


def split_store(block, columns, near_ref, far_ref, sent_ref):
    share = near_ref.shape[0]
    near_ref[:, columns] = block[:share].astype(near_ref.dtype)
    sent_ref[0, :, columns] = block[share : 2 * share].astype(sent_ref.dtype)
    far_ref[:, columns] = block[2 * share : 3 * share].astype(far_ref.dtype)
    sent_ref[1, :, columns] = block[3 * share :].astype(sent_ref.dtype)


def project_kernel(picker_ref, *refs):
    *piece_refs, w_ref, near_ref, far_ref, sent_ref, tiles, acc_ref, sems = refs
    count, depth = tiles.shape[0], tiles.shape[1]
    copies = [
        pltpu.make_async_copy(w_ref.at[pl.ds(i * depth, depth)], tiles.at[i], sems.at[i])
        for i in range(count)
    ]
    for copy in copies:
        copy.start()
    picker = picker_ref[...]
    for i in range(count):
        cut = slice(i * depth, (i + 1) * depth)
        rows = jnp.concatenate([piece_ref[:, cut] for piece_ref in piece_refs], axis=0)
        x = jnp.dot(picker, rows, preferred_element_type=jnp.float32).astype(jnp.bfloat16)
        copies[i].wait()
        for n in range(0, acc_ref.shape[1], 256):
            to = slice(n, n + 256)
            block = jnp.dot(x, tiles[i, :, to], preferred_element_type=jnp.float32)
            if i > 0:
                block += acc_ref[:, to]
            if i < count - 1:
                acc_ref[:, to] = block
            else:
                split_store(block, to, near_ref, far_ref, sent_ref)


def split_shapes(share, columns):
    return [
        jax.ShapeDtypeStruct((share, columns), jnp.float32),
        jax.ShapeDtypeStruct((share, columns), jnp.float32),
        jax.ShapeDtypeStruct((2, share, columns), jnp.bfloat16),
    ]


def project(picker, pieces, w):
    vmem = pl.BlockSpec(memory_space=pltpu.VMEM)
    depth, columns = w.shape
    tile = 512
    return pl.pallas_call(
        project_kernel,
        out_shape=split_shapes(picker.shape[0] // 4, columns),
        in_specs=[vmem] * (1 + len(pieces)) + [pl.BlockSpec(memory_space=pl.ANY)],
        out_specs=[vmem] * 3,
        scratch_shapes=[
            pltpu.VMEM((depth // tile, tile, columns), w.dtype),
            pltpu.VMEM((picker.shape[0], columns), jnp.float32),
            pltpu.SemaphoreType.DMA((depth // tile,)),
        ],
        compiler_params=pltpu.CompilerParams(vmem_limit_bytes=32 * 2**20),
        name="project",
    )(picker, *pieces, in_hbm(w))


def gate_kernel(x_ref, gate_ref, up_ref, near_ref, far_ref, sent_ref, tiles, sems, *, start):
    count, width = tiles.shape[0] // 2, tiles.shape[2]
    copies = []
    for i in range(2 * count):
        w_ref = gate_ref if i < count else up_ref
        at = pl.ds(start + (i % count) * width, width)
        copies.append(pltpu.make_async_copy(w_ref.at[:, at], tiles.at[i], sems.at[i]))
    for copy in copies:
        copy.start()
    x = x_ref[...]
    for i in range(2 * count):
        copies[i].wait()
        for n in range(0, width, 256):
            block = jnp.dot(x, tiles[i, :, n : n + 256], preferred_element_type=jnp.float32)
            at = i * width + n
            split_store(block, slice(at, at + 256), near_ref, far_ref, sent_ref)


def gate_and_up(x, w_gate, w_up, start, width):
    vmem = pl.BlockSpec(memory_space=pltpu.VMEM)
    hbm = pl.BlockSpec(memory_space=pl.ANY)
    tile = 768
    count = 2 * (width // tile)
    return pl.pallas_call(
        functools.partial(gate_kernel, start=start),
        out_shape=split_shapes(x.shape[0] // 4, 2 * width),
        in_specs=[vmem, hbm, hbm],
        out_specs=[vmem] * 3,
        scratch_shapes=[
            pltpu.VMEM((count, x.shape[1], tile), w_gate.dtype),
            pltpu.SemaphoreType.DMA((count,)),
        ],
        compiler_params=pltpu.CompilerParams(vmem_limit_bytes=32 * 2**20),
        name="gate_and_up",
    )(x, in_hbm(w_gate), in_hbm(w_up))


def in_vmem(w):
    return pltpu.with_memory_space_constraint(w, pltpu.VMEM)


def down_kernel(at_ref, *refs):
    refs, turned_ref = refs[:-1], refs[-1]
    refs, outs = refs[: -3 * PARTS], refs[-3 * PARTS :]
    *x_refs, w_ref = refs
    share, columns = outs[0].shape
    width = x_refs[0].shape[1]
    xs = [x_ref[...] for x_ref in x_refs]
    for p in range(PARTS):
        near_ref, far_ref, sent_ref = outs[3 * p : 3 * p + 3]
        for n in range(0, columns, 256):
            cut = slice(n, min(n + 256, columns))
            size = cut.stop - cut.start
            at = pl.ds(p * columns + n, size)
            block = sum(
                jnp.dot(x, w_ref[i * width : (i + 1) * width, at], preferred_element_type=jnp.float32)
                for i, x in enumerate(xs)
            )
            for j in range(4):
                turned_ref[jnp.bitwise_xor(at_ref[0], j), :, :size] = block[
                    j * share : (j + 1) * share
                ]
            near_ref[:, cut] = turned_ref[0, :, :size]
            sent_ref[0, :, cut] = turned_ref[1, :, :size].astype(sent_ref.dtype)
            far_ref[:, cut] = turned_ref[2, :, :size]
            sent_ref[1, :, cut] = turned_ref[3, :, :size].astype(sent_ref.dtype)


def down_project(at, xs, w):
    share = xs[0].shape[0] // 4
    vmem = pl.BlockSpec(memory_space=pltpu.VMEM)
    outs = pl.pallas_call(
        down_kernel,
        out_shape=split_shapes(share, w.shape[1] // PARTS) * PARTS,
        in_specs=[pl.BlockSpec(memory_space=pltpu.SMEM)] + [vmem] * (len(xs) + 1),
        out_specs=[vmem] * (3 * PARTS),
        scratch_shapes=[pltpu.VMEM((4, share, 256), jnp.float32)],
        compiler_params=pltpu.CompilerParams(vmem_limit_bytes=6 * 2**20),
        name="down_project",
    )(at.reshape(1), *xs, in_vmem(w))
    return [outs[3 * p : 3 * p + 3] for p in range(PARTS)]


def sum_first(sums):
    near, leaving = [], []
    for at_hand, far, sent in sums:
        came = lax.ppermute(sent, "ffn", swap_perm(4, 1))
        if leaving:
            came = tie(came, leaving[-1])
        near.append((at_hand, came[0]))
        leaving.append((far + came[1].astype(jnp.float32)).astype(jnp.bfloat16))
    return near, leaving


def sum_last(leaving, own, near):
    outs = []
    for p, last in enumerate(leaving):
        far = lax.ppermute(last, "ffn", swap_perm(4, 2))
        far = tie(far, outs[-1] if outs else leaving[-1])
        base = own[p].astype(jnp.float32) + near[p][0] + near[p][1].astype(jnp.float32)
        outs.append((lax.optimization_barrier(base) + far.astype(jnp.float32)).astype(jnp.bfloat16))
    return outs


def sum_direct(near, far, sent, own):
    far = far.astype(jnp.bfloat16)
    came = [
        lax.ppermute(x, "ffn", swap_perm(4, d)) for d, x in ((2, far), (3, sent[1]), (1, sent[0]))
    ]
    total = lax.optimization_barrier(own.astype(jnp.float32) + near)
    for part in came:
        total = total + part.astype(jnp.float32)
    return total.astype(jnp.bfloat16)


def paired_rows(
    pieces, row_picker, residual, turn, position, pages, w_out, w_gate, w_up, w_down
):
    count = row_picker.shape[0]
    share = count // 4
    columns = w_out.shape[1]
    step = w_gate.shape[1] // CHUNKS
    mine = lax.dynamic_slice_in_dim(residual, turn * share, share, 0)
    pieces, mine, pages = lax.optimization_barrier((pieces, mine, pages))
    landed = list(pages)
    landed[2] = lax.ppermute(pages[2], "attn", swap_perm(4, 2))
    near, far, sent = project(row_picker, pieces, w_out)
    sent, pages[1] = lax.optimization_barrier((sent, pages[1]))
    landed[1] = lax.ppermute(pages[1], "attn", swap_perm(4, 1))
    kept = sum_direct(near, far, sent, mine)
    came = {d: lax.ppermute(kept, "ffn", swap_perm(4, d)) for d in (2, 3, 1)}
    mixed = jnp.stack([kept, came[1], came[2], came[3]])
    mixed, landed[1], landed[2] = lax.optimization_barrier((mixed, landed[1], landed[2]))
    mixed, pages[3] = lax.optimization_barrier((mixed, pages[3]))
    landed[3] = lax.ppermute(pages[3], "attn", swap_perm(4, 3))
    rows = mixed.reshape(count, columns)

    stages = []
    for c in range(CHUNKS):
        near, far, sent = gate_and_up(rows, w_gate, w_up, c * step, step)
        if c == 0:
            sent, landed[3] = lax.optimization_barrier((sent, landed[3]))
        came, leaving = fold_first(sent, far, "attn")
        rows = tie(rows, leaving)
        stages.append((near, came, leaving))
    hiddens = []
    for c in range(CHUNKS):
        near, came, leaving = stages[c]
        sums = fold_last(leaving, (near, came), "attn")
        quarter = (jax.nn.silu(sums[:, :step]) * sums[:, step:]).astype(jnp.bfloat16)
        across = lax.ppermute(quarter, "attn", swap_perm(4, 2))
        if c + 1 < CHUNKS:
            across = tie(across, stages[c + 1][2])
        half = jnp.stack([quarter, across])
        other = lax.ppermute(half, "attn", swap_perm(4, 1))
        hidden = jnp.stack([half[0], other[0], half[1], other[1]]).reshape(count, step)
        hiddens.append(hidden)
    sums = down_project(position, hiddens, w_down)
    sums, landed = lax.optimization_barrier((sums, landed))
    kept = lax.dynamic_index_in_dim(mixed, position, 0, keepdims=False)
    outs = [sum_direct(*sums[0], kept)]
    return jnp.concatenate(outs, axis=1), landed


def settle(landed, incoming, pool_count, room_in, turn):
    came_usable = incoming < pool_count
    position_in = jnp.cumsum(came_usable.astype(jnp.int32)) - 1
    lanes = jnp.arange(room_in, dtype=jnp.int32)
    matches = jnp.logical_and(came_usable[None, :], position_in[None, :] == lanes[:, None])
    present = jnp.any(matches, axis=1)
    chosen = jnp.argmax(matches, axis=1)
    if turn is not None:
        pair_room = landed.shape[0] // 4
        chosen = jnp.bitwise_xor(chosen // pair_room, turn) * pair_room + chosen % pair_room
    arrived = jnp.take(landed, chosen, axis=0)
    return jnp.where(present[:, None, None], arrived, jnp.zeros_like(arrived))


def body(
    queries,
    new_kv,
    cache_pool,
    request_owner,
    block_req,
    migrate,
    residual_rows,
    w_out,
    w_gate,
    w_up,
    w_down,
):
    attn_count = lax.axis_size("attn")
    ffn_count = lax.axis_size("ffn")
    position = lax.axis_index("attn")
    ffn_position = lax.axis_index("ffn")
    req_dev = queries.shape[0]
    total_req = request_owner.shape[0]
    capacity = req_dev // 4
    slot_count = attn_count * capacity
    pool_count = cache_pool.shape[0]
    head_size = cache_pool.shape[2] // 2
    head_count = queries.shape[1] // head_size
    pair_room = migrate.shape[2]
    room_in = max(2, attn_count // 4) + 1
    paired = attn_count == 4 and ffn_count == 4

    owner_grid = request_owner.reshape(attn_count, req_dev)
    order = jnp.arange(req_dev, dtype=jnp.int32)
    earlier = order[None, :] < order[:, None]
    same = owner_grid[:, :, None] == owner_grid[:, None, :]
    order_rank = jnp.sum(jnp.logical_and(same, earlier[None]), axis=2)
    within = (jnp.arange(attn_count, dtype=jnp.int32)[:, None] * capacity + order_rank).reshape(-1)
    mine_owner = lax.dynamic_slice_in_dim(owner_grid, position, 1, 0)[0]
    mine_rank = lax.dynamic_slice_in_dim(order_rank, position, 1, 0)[0]
    target = jnp.bitwise_xor(mine_owner, position) if paired else mine_owner
    picker = (
        jnp.arange(slot_count, dtype=jnp.int32)[:, None] == (target * capacity + mine_rank)[None, :]
    ).astype(jnp.bfloat16)
    send = (
        jnp.dot(
            picker, jnp.concatenate([queries, new_kv], axis=1), preferred_element_type=jnp.float32
        )
        .astype(jnp.bfloat16)
        .reshape(attn_count, capacity, -1)
    )
    if paired:
        received = [send[0]] + [
            lax.ppermute(send[d], "attn", swap_perm(4, d)) for d in (2, 3, 1)
        ]
        distances = (0, 2, 3, 1)
    else:
        received = lax.all_to_all(send, "attn", split_axis=0, concat_axis=0, tiled=True)
        received = [received.reshape(slot_count, -1)]
        distances = (0,)
    my_moves = lax.dynamic_index_in_dim(migrate, position, 0, keepdims=False)
    numbers = jnp.concatenate(
        [
            position.astype(jnp.int32).reshape(1),
            lax.dynamic_index_in_dim(block_req, position, 0, keepdims=False),
            my_moves.reshape(-1),
            within,
        ]
    )
    attention, twin, *pages = attend(
        numbers,
        (attn_count, pair_room),
        received,
        distances,
        cache_pool,
        slot_count,
        head_count,
        head_size,
    )

    if paired:
        across = lax.ppermute(twin, "attn", swap_perm(4, 2))
        beside = lax.ppermute(twin, "attn", swap_perm(4, 1))
        corner = lax.ppermute(across, "attn", swap_perm(4, 1))
        everyone = [twin, across, beside, corner]
        distance = jnp.bitwise_xor(request_owner, position)
        place = distance // 2 + (distance % 2) * 2
    else:
        everyone = lax.all_gather(attention, "attn", axis=0, tiled=True)
        place = request_owner
    row_share = total_req // ffn_count
    row_of = (place * slot_count + within).reshape(ffn_count, row_share)
    if paired:
        turn = jnp.bitwise_xor(ffn_position, position)
        row_of = jnp.take(row_of, jnp.bitwise_xor(jnp.arange(4, dtype=jnp.int32), turn), axis=0)
    row_of = row_of.reshape(-1)
    row_picker = (
        row_of[:, None] == jnp.arange(attn_count * slot_count, dtype=jnp.int32)[None, :]
    ).astype(jnp.bfloat16)

    incoming = lax.dynamic_slice_in_dim(migrate, position, 1, 1)[:, 0, :].reshape(-1)
    if paired:
        ffn_out, landed = paired_rows(
            everyone, row_picker, residual_rows, turn, position, pages, w_out, w_gate, w_up, w_down
        )
        arrived = settle(jnp.concatenate(landed), incoming, pool_count, room_in, position)
        return (attention, arrived, ffn_out)

    sent_index = jnp.minimum(my_moves, pool_count - 1).reshape(-1)
    sent_blocks = jnp.take(cache_pool, sent_index, axis=0)
    sent_blocks = sent_blocks.reshape(attn_count, pair_room, cache_pool.shape[1], 2 * head_size)
    landed = lax.all_to_all(sent_blocks, "attn", split_axis=0, concat_axis=0, tiled=True)
    landed = landed.reshape(attn_count * pair_room, landed.shape[2], landed.shape[3])
    arrived = settle(landed, incoming, pool_count, room_in, None)

    ordered = jnp.dot(row_picker, everyone, preferred_element_type=jnp.float32).astype(jnp.bfloat16)
    columns = w_out.shape[1]
    projected = jnp.dot(ordered, w_out, preferred_element_type=jnp.float32).astype(jnp.bfloat16)
    parts = projected.reshape(ffn_count, row_share, columns)
    parts = lax.all_to_all(parts, "ffn", split_axis=0, concat_axis=0, tiled=True)
    mine = lax.dynamic_slice_in_dim(residual_rows, ffn_position * row_share, row_share, 0)
    kept = (mine.astype(jnp.float32) + jnp.sum(parts.astype(jnp.float32), axis=0)).astype(
        jnp.bfloat16
    )
    rows = lax.all_gather(kept, "ffn", axis=0, tiled=True)
    gate = jnp.dot(rows, w_gate, preferred_element_type=jnp.float32)
    up = jnp.dot(rows, w_up, preferred_element_type=jnp.float32)
    gate, up = lax.psum_scatter((gate, up), "attn", scatter_dimension=0, tiled=True)
    quarter = (jax.nn.silu(gate) * up).astype(jnp.bfloat16)
    hidden = lax.all_gather(quarter, "attn", axis=0, tiled=True)
    down = jnp.dot(hidden, w_down, preferred_element_type=jnp.float32).astype(jnp.bfloat16)
    shares = lax.all_to_all(
        down.reshape(ffn_count, row_share, columns), "ffn", split_axis=0, concat_axis=0, tiled=True
    )
    total = jnp.sum(shares.astype(jnp.float32), axis=0)
    ffn_out = (kept.astype(jnp.float32) + total).astype(jnp.bfloat16)
    return (attention, arrived, ffn_out)


def solution(mesh):
    placed = (
        P(("groups", "attn"), "ffn"),
        P(("groups", "attn"), None),
        P(("groups", "attn"), None, None),
        P("groups"),
        P("groups", None),
        P("groups", None, None),
        P("groups", "attn"),
        P("ffn", "attn"),
        P("attn", "ffn"),
        P("attn", "ffn"),
        P("ffn", "attn"),
    )
    return jax.shard_map(
        body,
        mesh=mesh,
        in_specs=placed,
        out_specs=(
            P(("groups", "attn"), "ffn"),
            P(("groups", "attn"), None, None),
            P(("groups", "ffn"), "attn"),
        ),
        check_vma=False,
    )
```

```python
import functools

import jax
import jax.numpy as jnp
from jax import lax
from jax.experimental import pallas as pl
from jax.experimental.pallas import tpu as pltpu
from jax.sharding import PartitionSpec as P

CHUNKS = 2
PARTS = 1


def attention_kernel(number_ref, *refs, distances):
    block_refs, refs = refs[: len(distances)], refs[len(distances) :]
    pool_ref, out_ref, twin_ref, *moved_refs, pages, move_sems, sems, q3, top_ref, den_ref, num_ref = refs
    page_count = pages.shape[0]
    place = number_ref[0]
    lanes = move_sems.shape[1]
    first = 1 + page_count + move_sems.shape[0] * lanes
    requests = number_ref.shape[0] - first
    heads, size = q3.shape[1], q3.shape[2]
    width = heads * size
    scale = size ** (-0.5)
    copies = [
        pltpu.make_async_copy(pool_ref.at[b], pages.at[b], sems.at[b]) for b in range(page_count)
    ]
    for copy in copies:
        copy.start()
    moves = []
    for d, moved_ref in enumerate(moved_refs):
        for m in range(moved_ref.shape[0]):
            page = number_ref[1 + page_count + jnp.bitwise_xor(place, d) * lanes + m]
            page = jnp.minimum(page, page_count - 1)
            moves.append(
                pltpu.make_async_copy(pool_ref.at[page], moved_ref.at[m], move_sems.at[d, m])
            )
    for move in moves:
        move.start()
    for i, block_ref in enumerate(block_refs):
        rows = block_ref.shape[0]
        at = pl.ds(jnp.bitwise_xor(place, distances[i]) * rows if len(distances) > 1 else 0, rows)
        for h in range(heads):
            q3[at, h, :] = block_ref[:, h * size : (h + 1) * size].astype(jnp.float32)
        key = block_ref[:, width : width + size].astype(jnp.float32)
        value = block_ref[:, width + size :].astype(jnp.float32)
        own = jnp.sum(q3[at] * key[:, None, :], axis=2, keepdims=True) * scale
        top_ref[at] = jnp.broadcast_to(own, (rows, heads, top_ref.shape[2]))
        num_ref[at] = jnp.broadcast_to(value[:, None, :], (rows, heads, size))
    den_ref[...] = jnp.ones_like(den_ref)
    terms = []
    slots = []
    for first_page in range(0, page_count, 7):
        group = range(first_page, min(first_page + 7, page_count))
        for b in group:
            copies[b].wait()
        live = []
        scores = []
        for b in group:
            request = number_ref[1 + b]
            slots.append(number_ref[first + jnp.minimum(request, requests - 1)])
            live.append(request < requests)
            q = q3[slots[b]].astype(jnp.bfloat16)
            scores.append(
                lax.dot_general(
                    q, pages[b, :, :size], (((1,), (1,)), ((), ())), preferred_element_type=jnp.float32
                )
                * scale
            )
        tops = [jnp.max(score, axis=1, keepdims=True) for score in scores]
        weights = [jnp.exp(score - top).astype(jnp.bfloat16) for score, top in zip(scores, tops)]
        for b, alive, top, weight in zip(group, live, tops, weights):
            total = jnp.sum(weight.astype(jnp.float32), axis=1, keepdims=True)
            summed = jnp.dot(weight, pages[b, :, size:], preferred_element_type=jnp.float32)
            terms.append((jnp.where(alive, top, -jnp.inf), total, summed))
    for b in range(page_count):
        top, total, summed = terms[b]
        slot = slots[b]
        old = top_ref[slot]
        top = jnp.broadcast_to(top, old.shape)
        new = jnp.maximum(old, top)
        keep = jnp.exp(old - new)
        take = jnp.exp(top - new)
        top_ref[slot] = new
        den_ref[slot] = den_ref[slot] * keep + take * total
        num_ref[slot] = num_ref[slot] * keep[:, :1] + take[:, :1] * summed
    for h in range(heads):
        cut = slice(h * size, (h + 1) * size)
        result = (num_ref[:, h, :] / den_ref[:, h, :1]).astype(out_ref.dtype)
        out_ref[:, cut] = result
        twin_ref[:, cut] = result
    for move in moves:
        move.wait()


def in_hbm(x):
    return pltpu.with_memory_space_constraint(x, pltpu.HBM)


def attend(numbers, room, received, distances, cache_pool, slots, heads, size):
    page_count = cache_pool.shape[0]
    moved = jax.ShapeDtypeStruct((room[1],) + cache_pool.shape[1:], cache_pool.dtype)
    moved = [moved] * (len(distances) if len(distances) > 1 else 0)
    smem = pl.BlockSpec(memory_space=pltpu.SMEM)
    vmem = pl.BlockSpec(memory_space=pltpu.VMEM)
    return pl.pallas_call(
        functools.partial(attention_kernel, distances=distances),
        out_shape=[jax.ShapeDtypeStruct((slots, heads * size), jnp.bfloat16)] * 2 + moved,
        in_specs=[smem] + [vmem] * len(received) + [pl.BlockSpec(memory_space=pl.ANY)],
        out_specs=[vmem, vmem] + [pl.BlockSpec(memory_space=pl.ANY)] * len(moved),
        scratch_shapes=[
            pltpu.VMEM(cache_pool.shape, jnp.bfloat16),
            pltpu.SemaphoreType.DMA(room),
            pltpu.SemaphoreType.DMA((page_count,)),
            pltpu.VMEM((slots, heads, size), jnp.float32),
            pltpu.VMEM((slots, heads, 128), jnp.float32),
            pltpu.VMEM((slots, heads, 128), jnp.float32),
            pltpu.VMEM((slots, heads, size), jnp.float32),
        ],
        compiler_params=pltpu.CompilerParams(vmem_limit_bytes=24 * 2**20),
        name="attention",
    )(numbers, *received, in_hbm(cache_pool))


def swap_perm(count, bit):
    return [(i, i ^ bit) for i in range(count)]


def tie(x, *others):
    return lax.optimization_barrier((x, others))[0]


def fold_first(sent, far, axis):
    came = lax.ppermute(sent, axis, swap_perm(4, 1))
    return came[0], (far + came[1].astype(jnp.float32)).astype(jnp.bfloat16)


def fold_last(leaving, own, axis):
    far = lax.ppermute(leaving, axis, swap_perm(4, 2))
    total = own[0].astype(jnp.float32)
    for part in own[1:]:
        total = total + part.astype(jnp.float32)
    return lax.optimization_barrier(total) + far.astype(jnp.float32)


def split_store(block, columns, near_ref, far_ref, sent_ref):
    share = near_ref.shape[0]
    near_ref[:, columns] = block[:share].astype(near_ref.dtype)
    sent_ref[0, :, columns] = block[share : 2 * share].astype(sent_ref.dtype)
    far_ref[:, columns] = block[2 * share : 3 * share].astype(far_ref.dtype)
    sent_ref[1, :, columns] = block[3 * share :].astype(sent_ref.dtype)


def project_kernel(picker_ref, *refs):
    *piece_refs, w_ref, near_ref, far_ref, sent_ref, tiles, acc_ref, sems = refs
    count, depth = tiles.shape[0], tiles.shape[1]
    copies = [
        pltpu.make_async_copy(w_ref.at[pl.ds(i * depth, depth)], tiles.at[i], sems.at[i])
        for i in range(count)
    ]
    for copy in copies:
        copy.start()
    picker = picker_ref[...]
    for i in range(count):
        cut = slice(i * depth, (i + 1) * depth)
        rows = jnp.concatenate([piece_ref[:, cut] for piece_ref in piece_refs], axis=0)
        x = jnp.dot(picker, rows, preferred_element_type=jnp.float32).astype(jnp.bfloat16)
        copies[i].wait()
        for n in range(0, acc_ref.shape[1], 256):
            to = slice(n, n + 256)
            block = jnp.dot(x, tiles[i, :, to], preferred_element_type=jnp.float32)
            if i > 0:
                block += acc_ref[:, to]
            if i < count - 1:
                acc_ref[:, to] = block
            else:
                split_store(block, to, near_ref, far_ref, sent_ref)


def split_shapes(share, columns):
    return [
        jax.ShapeDtypeStruct((share, columns), jnp.float32),
        jax.ShapeDtypeStruct((share, columns), jnp.float32),
        jax.ShapeDtypeStruct((2, share, columns), jnp.bfloat16),
    ]


def project(picker, pieces, w):
    vmem = pl.BlockSpec(memory_space=pltpu.VMEM)
    depth, columns = w.shape
    tile = 512
    return pl.pallas_call(
        project_kernel,
        out_shape=split_shapes(picker.shape[0] // 4, columns),
        in_specs=[vmem] * (1 + len(pieces)) + [pl.BlockSpec(memory_space=pl.ANY)],
        out_specs=[vmem] * 3,
        scratch_shapes=[
            pltpu.VMEM((depth // tile, tile, columns), w.dtype),
            pltpu.VMEM((picker.shape[0], columns), jnp.float32),
            pltpu.SemaphoreType.DMA((depth // tile,)),
        ],
        compiler_params=pltpu.CompilerParams(vmem_limit_bytes=32 * 2**20),
        name="project",
    )(picker, *pieces, in_hbm(w))


def gate_kernel(x_ref, gate_ref, up_ref, near_ref, far_ref, sent_ref, tiles, sems, *, start):
    count, width = tiles.shape[0] // 2, tiles.shape[2]
    copies = []
    for i in range(2 * count):
        w_ref = gate_ref if i < count else up_ref
        at = pl.ds(start + (i % count) * width, width)
        copies.append(pltpu.make_async_copy(w_ref.at[:, at], tiles.at[i], sems.at[i]))
    for copy in copies:
        copy.start()
    x = x_ref[...]
    for i in range(2 * count):
        copies[i].wait()
        for n in range(0, width, 256):
            block = jnp.dot(x, tiles[i, :, n : n + 256], preferred_element_type=jnp.float32)
            at = i * width + n
            split_store(block, slice(at, at + 256), near_ref, far_ref, sent_ref)


def gate_and_up(x, w_gate, w_up, start, width):
    vmem = pl.BlockSpec(memory_space=pltpu.VMEM)
    hbm = pl.BlockSpec(memory_space=pl.ANY)
    tile = 768
    count = 2 * (width // tile)
    return pl.pallas_call(
        functools.partial(gate_kernel, start=start),
        out_shape=split_shapes(x.shape[0] // 4, 2 * width),
        in_specs=[vmem, hbm, hbm],
        out_specs=[vmem] * 3,
        scratch_shapes=[
            pltpu.VMEM((count, x.shape[1], tile), w_gate.dtype),
            pltpu.SemaphoreType.DMA((count,)),
        ],
        compiler_params=pltpu.CompilerParams(vmem_limit_bytes=32 * 2**20),
        name="gate_and_up",
    )(x, in_hbm(w_gate), in_hbm(w_up))


def in_vmem(w):
    return pltpu.with_memory_space_constraint(w, pltpu.VMEM)


def down_kernel(at_ref, *refs):
    refs, turned_ref = refs[:-1], refs[-1]
    refs, outs = refs[: -3 * PARTS], refs[-3 * PARTS :]
    *x_refs, w_ref = refs
    share, columns = outs[0].shape
    width = x_refs[0].shape[1]
    xs = [x_ref[...] for x_ref in x_refs]
    for p in range(PARTS):
        near_ref, far_ref, sent_ref = outs[3 * p : 3 * p + 3]
        for n in range(0, columns, 256):
            cut = slice(n, min(n + 256, columns))
            size = cut.stop - cut.start
            at = pl.ds(p * columns + n, size)
            block = sum(
                jnp.dot(x, w_ref[i * width : (i + 1) * width, at], preferred_element_type=jnp.float32)
                for i, x in enumerate(xs)
            )
            for j in range(4):
                turned_ref[jnp.bitwise_xor(at_ref[0], j), :, :size] = block[
                    j * share : (j + 1) * share
                ]
            near_ref[:, cut] = turned_ref[0, :, :size]
            sent_ref[0, :, cut] = turned_ref[1, :, :size].astype(sent_ref.dtype)
            far_ref[:, cut] = turned_ref[2, :, :size]
            sent_ref[1, :, cut] = turned_ref[3, :, :size].astype(sent_ref.dtype)


def down_project(at, xs, w):
    share = xs[0].shape[0] // 4
    vmem = pl.BlockSpec(memory_space=pltpu.VMEM)
    outs = pl.pallas_call(
        down_kernel,
        out_shape=split_shapes(share, w.shape[1] // PARTS) * PARTS,
        in_specs=[pl.BlockSpec(memory_space=pltpu.SMEM)] + [vmem] * (len(xs) + 1),
        out_specs=[vmem] * (3 * PARTS),
        scratch_shapes=[pltpu.VMEM((4, share, 256), jnp.float32)],
        compiler_params=pltpu.CompilerParams(vmem_limit_bytes=6 * 2**20),
        name="down_project",
    )(at.reshape(1), *xs, in_vmem(w))
    return [outs[3 * p : 3 * p + 3] for p in range(PARTS)]


def sum_direct(near, far, sent, own):
    far = far.astype(jnp.bfloat16)
    came = [
        lax.ppermute(x, "ffn", swap_perm(4, d)) for d, x in ((2, far), (3, sent[1]), (1, sent[0]))
    ]
    total = lax.optimization_barrier(own.astype(jnp.float32) + near)
    for part in came:
        total = total + part.astype(jnp.float32)
    return total.astype(jnp.bfloat16)


def paired_rows(
    pieces, row_picker, residual, turn, position, pages, w_out, w_gate, w_up, w_down
):
    count = row_picker.shape[0]
    share = count // 4
    columns = w_out.shape[1]
    step = w_gate.shape[1] // CHUNKS
    mine = lax.dynamic_slice_in_dim(residual, turn * share, share, 0)
    pieces, mine, pages = lax.optimization_barrier((pieces, mine, pages))
    landed = list(pages)
    near, far, sent = project(row_picker, pieces, w_out)
    sent, pages = lax.optimization_barrier((sent, pages))
    landed[2] = lax.ppermute(pages[2], "attn", swap_perm(4, 2))
    landed[1] = lax.ppermute(pages[1], "attn", swap_perm(4, 1))
    kept = sum_direct(near, far, sent, mine)
    kept, landed[1], landed[2], pages[3] = lax.optimization_barrier(
        (kept, landed[1], landed[2], pages[3])
    )
    landed[3] = lax.ppermute(pages[3], "attn", swap_perm(4, 3))
    came = {d: lax.ppermute(kept, "ffn", swap_perm(4, d)) for d in (2, 3, 1)}
    mixed = jnp.stack([kept, came[1], came[2], came[3]])
    mixed, landed[3] = lax.optimization_barrier((mixed, landed[3]))
    rows = mixed.reshape(count, columns)

    stages = []
    for c in range(CHUNKS):
        near, far, sent = gate_and_up(rows, w_gate, w_up, c * step, step)
        came, leaving = fold_first(sent, far, "attn")
        rows = tie(rows, leaving)
        stages.append((near, came, leaving))
    hiddens = []
    for c in range(CHUNKS):
        near, came, leaving = stages[c]
        sums = fold_last(leaving, (near, came), "attn")
        quarter = (jax.nn.silu(sums[:, :step]) * sums[:, step:]).astype(jnp.bfloat16)
        across = lax.ppermute(quarter, "attn", swap_perm(4, 2))
        if c + 1 < CHUNKS:
            across = tie(across, stages[c + 1][2])
        half = jnp.stack([quarter, across])
        other = lax.ppermute(half, "attn", swap_perm(4, 1))
        hidden = jnp.stack([half[0], other[0], half[1], other[1]]).reshape(count, step)
        hiddens.append(hidden)
    sums = down_project(position, hiddens, w_down)
    sums, landed = lax.optimization_barrier((sums, landed))
    kept = lax.dynamic_index_in_dim(mixed, position, 0, keepdims=False)
    outs = [sum_direct(*sums[0], kept)]
    return jnp.concatenate(outs, axis=1), landed


def settle(landed, incoming, pool_count, room_in, turn):
    came_usable = incoming < pool_count
    position_in = jnp.cumsum(came_usable.astype(jnp.int32)) - 1
    lanes = jnp.arange(room_in, dtype=jnp.int32)
    matches = jnp.logical_and(came_usable[None, :], position_in[None, :] == lanes[:, None])
    present = jnp.any(matches, axis=1)
    chosen = jnp.argmax(matches, axis=1)
    if turn is not None:
        pair_room = landed.shape[0] // 4
        chosen = jnp.bitwise_xor(chosen // pair_room, turn) * pair_room + chosen % pair_room
    arrived = jnp.take(landed, chosen, axis=0)
    return jnp.where(present[:, None, None], arrived, jnp.zeros_like(arrived))


def body(
    queries,
    new_kv,
    cache_pool,
    request_owner,
    block_req,
    migrate,
    residual_rows,
    w_out,
    w_gate,
    w_up,
    w_down,
):
    attn_count = lax.axis_size("attn")
    ffn_count = lax.axis_size("ffn")
    position = lax.axis_index("attn")
    ffn_position = lax.axis_index("ffn")
    req_dev = queries.shape[0]
    total_req = request_owner.shape[0]
    capacity = req_dev // 4
    slot_count = attn_count * capacity
    pool_count = cache_pool.shape[0]
    head_size = cache_pool.shape[2] // 2
    head_count = queries.shape[1] // head_size
    pair_room = migrate.shape[2]
    room_in = max(2, attn_count // 4) + 1
    paired = attn_count == 4 and ffn_count == 4

    owner_grid = request_owner.reshape(attn_count, req_dev)
    order = jnp.arange(req_dev, dtype=jnp.int32)
    earlier = order[None, :] < order[:, None]
    same = owner_grid[:, :, None] == owner_grid[:, None, :]
    order_rank = jnp.sum(jnp.logical_and(same, earlier[None]), axis=2)
    within = (jnp.arange(attn_count, dtype=jnp.int32)[:, None] * capacity + order_rank).reshape(-1)
    mine_owner = lax.dynamic_slice_in_dim(owner_grid, position, 1, 0)[0]
    mine_rank = lax.dynamic_slice_in_dim(order_rank, position, 1, 0)[0]
    target = jnp.bitwise_xor(mine_owner, position) if paired else mine_owner
    picker = (
        jnp.arange(slot_count, dtype=jnp.int32)[:, None] == (target * capacity + mine_rank)[None, :]
    ).astype(jnp.bfloat16)
    send = (
        jnp.dot(
            picker, jnp.concatenate([queries, new_kv], axis=1), preferred_element_type=jnp.float32
        )
        .astype(jnp.bfloat16)
        .reshape(attn_count, capacity, -1)
    )
    if paired:
        received = [send[0]] + [
            lax.ppermute(send[d], "attn", swap_perm(4, d)) for d in (2, 3, 1)
        ]
        distances = (0, 2, 3, 1)
    else:
        received = lax.all_to_all(send, "attn", split_axis=0, concat_axis=0, tiled=True)
        received = [received.reshape(slot_count, -1)]
        distances = (0,)
    my_moves = lax.dynamic_index_in_dim(migrate, position, 0, keepdims=False)
    numbers = jnp.concatenate(
        [
            position.astype(jnp.int32).reshape(1),
            lax.dynamic_index_in_dim(block_req, position, 0, keepdims=False),
            my_moves.reshape(-1),
            within,
        ]
    )
    attention, twin, *pages = attend(
        numbers,
        (attn_count, pair_room),
        received,
        distances,
        cache_pool,
        slot_count,
        head_count,
        head_size,
    )

    if paired:
        across = lax.ppermute(twin, "attn", swap_perm(4, 2))
        beside = lax.ppermute(twin, "attn", swap_perm(4, 1))
        corner = lax.ppermute(across, "attn", swap_perm(4, 1))
        everyone = [twin, across, beside, corner]
        distance = jnp.bitwise_xor(request_owner, position)
        place = distance // 2 + (distance % 2) * 2
    else:
        everyone = lax.all_gather(attention, "attn", axis=0, tiled=True)
        place = request_owner
    row_share = total_req // ffn_count
    row_of = (place * slot_count + within).reshape(ffn_count, row_share)
    if paired:
        turn = jnp.bitwise_xor(ffn_position, position)
        row_of = jnp.take(row_of, jnp.bitwise_xor(jnp.arange(4, dtype=jnp.int32), turn), axis=0)
    row_of = row_of.reshape(-1)
    row_picker = (
        row_of[:, None] == jnp.arange(attn_count * slot_count, dtype=jnp.int32)[None, :]
    ).astype(jnp.bfloat16)

    incoming = lax.dynamic_slice_in_dim(migrate, position, 1, 1)[:, 0, :].reshape(-1)
    if paired:
        ffn_out, landed = paired_rows(
            everyone, row_picker, residual_rows, turn, position, pages, w_out, w_gate, w_up, w_down
        )
        arrived = settle(jnp.concatenate(landed), incoming, pool_count, room_in, position)
        return (attention, arrived, ffn_out)

    sent_index = jnp.minimum(my_moves, pool_count - 1).reshape(-1)
    sent_blocks = jnp.take(cache_pool, sent_index, axis=0)
    sent_blocks = sent_blocks.reshape(attn_count, pair_room, cache_pool.shape[1], 2 * head_size)
    landed = lax.all_to_all(sent_blocks, "attn", split_axis=0, concat_axis=0, tiled=True)
    landed = landed.reshape(attn_count * pair_room, landed.shape[2], landed.shape[3])
    arrived = settle(landed, incoming, pool_count, room_in, None)

    ordered = jnp.dot(row_picker, everyone, preferred_element_type=jnp.float32).astype(jnp.bfloat16)
    columns = w_out.shape[1]
    projected = jnp.dot(ordered, w_out, preferred_element_type=jnp.float32).astype(jnp.bfloat16)
    parts = projected.reshape(ffn_count, row_share, columns)
    parts = lax.all_to_all(parts, "ffn", split_axis=0, concat_axis=0, tiled=True)
    mine = lax.dynamic_slice_in_dim(residual_rows, ffn_position * row_share, row_share, 0)
    kept = (mine.astype(jnp.float32) + jnp.sum(parts.astype(jnp.float32), axis=0)).astype(
        jnp.bfloat16
    )
    rows = lax.all_gather(kept, "ffn", axis=0, tiled=True)
    gate = jnp.dot(rows, w_gate, preferred_element_type=jnp.float32)
    up = jnp.dot(rows, w_up, preferred_element_type=jnp.float32)
    gate, up = lax.psum_scatter((gate, up), "attn", scatter_dimension=0, tiled=True)
    quarter = (jax.nn.silu(gate) * up).astype(jnp.bfloat16)
    hidden = lax.all_gather(quarter, "attn", axis=0, tiled=True)
    down = jnp.dot(hidden, w_down, preferred_element_type=jnp.float32).astype(jnp.bfloat16)
    shares = lax.all_to_all(
        down.reshape(ffn_count, row_share, columns), "ffn", split_axis=0, concat_axis=0, tiled=True
    )
    total = jnp.sum(shares.astype(jnp.float32), axis=0)
    ffn_out = (kept.astype(jnp.float32) + total).astype(jnp.bfloat16)
    return (attention, arrived, ffn_out)


def solution(mesh):
    placed = (
        P(("groups", "attn"), "ffn"),
        P(("groups", "attn"), None),
        P(("groups", "attn"), None, None),
        P("groups"),
        P("groups", None),
        P("groups", None, None),
        P("groups", "attn"),
        P("ffn", "attn"),
        P("attn", "ffn"),
        P("attn", "ffn"),
        P("ffn", "attn"),
    )
    return jax.shard_map(
        body,
        mesh=mesh,
        in_specs=placed,
        out_specs=(
            P(("groups", "attn"), "ffn"),
            P(("groups", "attn"), None, None),
            P(("groups", "ffn"), "attn"),
        ),
        check_vma=False,
    )
```

```python
import functools

import jax
import jax.numpy as jnp
from jax import lax
from jax.experimental import pallas as pl
from jax.experimental.pallas import tpu as pltpu
from jax.sharding import PartitionSpec as P

CHUNKS = 2
PARTS = 1


def attention_kernel(number_ref, *refs, distances):
    block_refs, refs = refs[: len(distances)], refs[len(distances) :]
    pool_ref, out_ref, twin_ref, *moved_refs, pages, move_sems, sems, q3, top_ref, den_ref, num_ref = refs
    page_count = pages.shape[0]
    place = number_ref[0]
    lanes = move_sems.shape[1]
    first = 1 + page_count + move_sems.shape[0] * lanes
    requests = number_ref.shape[0] - first
    heads, size = q3.shape[1], q3.shape[2]
    width = heads * size
    scale = size ** (-0.5)
    copies = [
        pltpu.make_async_copy(pool_ref.at[b], pages.at[b], sems.at[b]) for b in range(page_count)
    ]
    for copy in copies:
        copy.start()
    moves = []
    for d, moved_ref in enumerate(moved_refs):
        for m in range(moved_ref.shape[0]):
            page = number_ref[1 + page_count + jnp.bitwise_xor(place, d) * lanes + m]
            page = jnp.minimum(page, page_count - 1)
            moves.append(
                pltpu.make_async_copy(pool_ref.at[page], moved_ref.at[m], move_sems.at[d, m])
            )
    for move in moves:
        move.start()
    for i, block_ref in enumerate(block_refs):
        rows = block_ref.shape[0]
        at = pl.ds(jnp.bitwise_xor(place, distances[i]) * rows if len(distances) > 1 else 0, rows)
        for h in range(heads):
            q3[at, h, :] = block_ref[:, h * size : (h + 1) * size].astype(jnp.float32)
        key = block_ref[:, width : width + size].astype(jnp.float32)
        value = block_ref[:, width + size :].astype(jnp.float32)
        own = jnp.sum(q3[at] * key[:, None, :], axis=2, keepdims=True) * scale
        top_ref[at] = jnp.broadcast_to(own, (rows, heads, top_ref.shape[2]))
        num_ref[at] = jnp.broadcast_to(value[:, None, :], (rows, heads, size))
    den_ref[...] = jnp.ones_like(den_ref)
    terms = []
    slots = []
    for first_page in range(0, page_count, 7):
        group = range(first_page, min(first_page + 7, page_count))
        for b in group:
            copies[b].wait()
        live = []
        scores = []
        for b in group:
            request = number_ref[1 + b]
            slots.append(number_ref[first + jnp.minimum(request, requests - 1)])
            live.append(request < requests)
            q = q3[slots[b]].astype(jnp.bfloat16)
            scores.append(
                lax.dot_general(
                    q, pages[b, :, :size], (((1,), (1,)), ((), ())), preferred_element_type=jnp.float32
                )
                * scale
            )
        tops = [jnp.max(score, axis=1, keepdims=True) for score in scores]
        weights = [jnp.exp(score - top).astype(jnp.bfloat16) for score, top in zip(scores, tops)]
        for b, alive, top, weight in zip(group, live, tops, weights):
            total = jnp.sum(weight.astype(jnp.float32), axis=1, keepdims=True)
            summed = jnp.dot(weight, pages[b, :, size:], preferred_element_type=jnp.float32)
            terms.append((jnp.where(alive, top, -jnp.inf), total, summed))
    for b in range(page_count):
        top, total, summed = terms[b]
        slot = slots[b]
        old = top_ref[slot]
        top = jnp.broadcast_to(top, old.shape)
        new = jnp.maximum(old, top)
        keep = jnp.exp(old - new)
        take = jnp.exp(top - new)
        top_ref[slot] = new
        den_ref[slot] = den_ref[slot] * keep + take * total
        num_ref[slot] = num_ref[slot] * keep[:, :1] + take[:, :1] * summed
    for h in range(heads):
        cut = slice(h * size, (h + 1) * size)
        result = (num_ref[:, h, :] / den_ref[:, h, :1]).astype(out_ref.dtype)
        out_ref[:, cut] = result
        twin_ref[:, cut] = result
    for move in moves:
        move.wait()


def in_hbm(x):
    return pltpu.with_memory_space_constraint(x, pltpu.HBM)


def attend(numbers, room, received, distances, cache_pool, slots, heads, size):
    page_count = cache_pool.shape[0]
    moved = jax.ShapeDtypeStruct((room[1],) + cache_pool.shape[1:], cache_pool.dtype)
    moved = [moved] * (len(distances) if len(distances) > 1 else 0)
    smem = pl.BlockSpec(memory_space=pltpu.SMEM)
    vmem = pl.BlockSpec(memory_space=pltpu.VMEM)
    return pl.pallas_call(
        functools.partial(attention_kernel, distances=distances),
        out_shape=[jax.ShapeDtypeStruct((slots, heads * size), jnp.bfloat16)] * 2 + moved,
        in_specs=[smem] + [vmem] * len(received) + [pl.BlockSpec(memory_space=pl.ANY)],
        out_specs=[vmem, vmem] + [pl.BlockSpec(memory_space=pl.ANY)] * len(moved),
        scratch_shapes=[
            pltpu.VMEM(cache_pool.shape, jnp.bfloat16),
            pltpu.SemaphoreType.DMA(room),
            pltpu.SemaphoreType.DMA((page_count,)),
            pltpu.VMEM((slots, heads, size), jnp.float32),
            pltpu.VMEM((slots, heads, 128), jnp.float32),
            pltpu.VMEM((slots, heads, 128), jnp.float32),
            pltpu.VMEM((slots, heads, size), jnp.float32),
        ],
        compiler_params=pltpu.CompilerParams(vmem_limit_bytes=12 * 2**20),
        name="attention",
    )(numbers, *received, in_hbm(cache_pool))


def swap_perm(count, bit):
    return [(i, i ^ bit) for i in range(count)]


def tie(x, *others):
    return lax.optimization_barrier((x, others))[0]


def fold_first(sent, far, axis):
    came = lax.ppermute(sent, axis, swap_perm(4, 1))
    return came[0], (far + came[1].astype(jnp.float32)).astype(jnp.bfloat16)


def fold_last(leaving, own, axis):
    far = lax.ppermute(leaving, axis, swap_perm(4, 2))
    total = own[0].astype(jnp.float32)
    for part in own[1:]:
        total = total + part.astype(jnp.float32)
    return lax.optimization_barrier(total) + far.astype(jnp.float32)


def split_store(block, columns, near_ref, far_ref, sent_ref):
    share = near_ref.shape[0]
    near_ref[:, columns] = block[:share].astype(near_ref.dtype)
    sent_ref[0, :, columns] = block[share : 2 * share].astype(sent_ref.dtype)
    far_ref[:, columns] = block[2 * share : 3 * share].astype(far_ref.dtype)
    sent_ref[1, :, columns] = block[3 * share :].astype(sent_ref.dtype)


def project_kernel(picker_ref, *refs):
    *piece_refs, w_ref, near_ref, far_ref, sent_ref, tiles, acc_ref, sems = refs
    count, depth = tiles.shape[0], tiles.shape[1]
    copies = [
        pltpu.make_async_copy(w_ref.at[pl.ds(i * depth, depth)], tiles.at[i], sems.at[i])
        for i in range(count)
    ]
    for copy in copies:
        copy.start()
    picker = picker_ref[...]
    for i in range(count):
        cut = slice(i * depth, (i + 1) * depth)
        rows = jnp.concatenate([piece_ref[:, cut] for piece_ref in piece_refs], axis=0)
        x = jnp.dot(picker, rows, preferred_element_type=jnp.float32).astype(jnp.bfloat16)
        copies[i].wait()
        for n in range(0, acc_ref.shape[1], 256):
            to = slice(n, n + 256)
            block = jnp.dot(x, tiles[i, :, to], preferred_element_type=jnp.float32)
            if i > 0:
                block += acc_ref[:, to]
            if i < count - 1:
                acc_ref[:, to] = block
            else:
                split_store(block, to, near_ref, far_ref, sent_ref)


def split_shapes(share, columns):
    return [
        jax.ShapeDtypeStruct((share, columns), jnp.float32),
        jax.ShapeDtypeStruct((share, columns), jnp.float32),
        jax.ShapeDtypeStruct((2, share, columns), jnp.bfloat16),
    ]


def project(picker, pieces, w):
    vmem = pl.BlockSpec(memory_space=pltpu.VMEM)
    depth, columns = w.shape
    tile = 512
    return pl.pallas_call(
        project_kernel,
        out_shape=split_shapes(picker.shape[0] // 4, columns),
        in_specs=[vmem] * (1 + len(pieces)) + [pl.BlockSpec(memory_space=pl.ANY)],
        out_specs=[vmem] * 3,
        scratch_shapes=[
            pltpu.VMEM((depth // tile, tile, columns), w.dtype),
            pltpu.VMEM((picker.shape[0], columns), jnp.float32),
            pltpu.SemaphoreType.DMA((depth // tile,)),
        ],
        compiler_params=pltpu.CompilerParams(vmem_limit_bytes=20 * 2**20),
        name="project",
    )(picker, *pieces, in_hbm(w))


def gate_kernel(x_ref, gate_ref, up_ref, near_ref, far_ref, sent_ref, tiles, sems, *, start):
    count, width = tiles.shape[0] // 2, tiles.shape[2]
    copies = []
    for i in range(2 * count):
        w_ref = gate_ref if i < count else up_ref
        at = pl.ds(start + (i % count) * width, width)
        copies.append(pltpu.make_async_copy(w_ref.at[:, at], tiles.at[i], sems.at[i]))
    for copy in copies:
        copy.start()
    x = x_ref[...]
    for i in range(2 * count):
        copies[i].wait()
        for n in range(0, width, 256):
            block = jnp.dot(x, tiles[i, :, n : n + 256], preferred_element_type=jnp.float32)
            at = i * width + n
            split_store(block, slice(at, at + 256), near_ref, far_ref, sent_ref)


def gate_and_up(x, w_gate, w_up, start, width):
    vmem = pl.BlockSpec(memory_space=pltpu.VMEM)
    hbm = pl.BlockSpec(memory_space=pl.ANY)
    tile = 768
    count = 2 * (width // tile)
    return pl.pallas_call(
        functools.partial(gate_kernel, start=start),
        out_shape=split_shapes(x.shape[0] // 4, 2 * width),
        in_specs=[vmem, hbm, hbm],
        out_specs=[vmem] * 3,
        scratch_shapes=[
            pltpu.VMEM((count, x.shape[1], tile), w_gate.dtype),
            pltpu.SemaphoreType.DMA((count,)),
        ],
        compiler_params=pltpu.CompilerParams(vmem_limit_bytes=20 * 2**20),
        name="gate_and_up",
    )(x, in_hbm(w_gate), in_hbm(w_up))


def in_vmem(w):
    return pltpu.with_memory_space_constraint(w, pltpu.VMEM)


def down_kernel(at_ref, *refs):
    refs, turned_ref = refs[:-1], refs[-1]
    refs, outs = refs[: -3 * PARTS], refs[-3 * PARTS :]
    *x_refs, w_ref = refs
    share, columns = outs[0].shape
    width = x_refs[0].shape[1]
    xs = [x_ref[...] for x_ref in x_refs]
    for p in range(PARTS):
        near_ref, far_ref, sent_ref = outs[3 * p : 3 * p + 3]
        for n in range(0, columns, 256):
            cut = slice(n, min(n + 256, columns))
            size = cut.stop - cut.start
            at = pl.ds(p * columns + n, size)
            block = sum(
                jnp.dot(x, w_ref[i * width : (i + 1) * width, at], preferred_element_type=jnp.float32)
                for i, x in enumerate(xs)
            )
            for j in range(4):
                turned_ref[jnp.bitwise_xor(at_ref[0], j), :, :size] = block[
                    j * share : (j + 1) * share
                ]
            near_ref[:, cut] = turned_ref[0, :, :size]
            sent_ref[0, :, cut] = turned_ref[1, :, :size].astype(sent_ref.dtype)
            far_ref[:, cut] = turned_ref[2, :, :size]
            sent_ref[1, :, cut] = turned_ref[3, :, :size].astype(sent_ref.dtype)


def down_project(at, xs, w):
    share = xs[0].shape[0] // 4
    vmem = pl.BlockSpec(memory_space=pltpu.VMEM)
    outs = pl.pallas_call(
        down_kernel,
        out_shape=split_shapes(share, w.shape[1] // PARTS) * PARTS,
        in_specs=[pl.BlockSpec(memory_space=pltpu.SMEM)] + [vmem] * (len(xs) + 1),
        out_specs=[vmem] * (3 * PARTS),
        scratch_shapes=[pltpu.VMEM((4, share, 256), jnp.float32)],
        compiler_params=pltpu.CompilerParams(vmem_limit_bytes=6 * 2**20),
        name="down_project",
    )(at.reshape(1), *xs, in_vmem(w))
    return [outs[3 * p : 3 * p + 3] for p in range(PARTS)]


def sum_direct(near, far, sent, own):
    far = far.astype(jnp.bfloat16)
    came = [
        lax.ppermute(x, "ffn", swap_perm(4, d)) for d, x in ((2, far), (3, sent[1]), (1, sent[0]))
    ]
    total = lax.optimization_barrier(own.astype(jnp.float32) + near)
    for part in came:
        total = total + part.astype(jnp.float32)
    return total.astype(jnp.bfloat16)


def paired_rows(
    pieces, row_picker, residual, turn, position, pages, w_out, w_gate, w_up, w_down
):
    count = row_picker.shape[0]
    share = count // 4
    columns = w_out.shape[1]
    step = w_gate.shape[1] // CHUNKS
    mine = lax.dynamic_slice_in_dim(residual, turn * share, share, 0)
    pieces, mine, pages = lax.optimization_barrier((pieces, mine, pages))
    landed = list(pages)
    near, far, sent = project(row_picker, pieces, w_out)
    sent, pages = lax.optimization_barrier((sent, pages))
    landed[2] = lax.ppermute(pages[2], "attn", swap_perm(4, 2))
    landed[1] = lax.ppermute(pages[1], "attn", swap_perm(4, 1))
    kept = sum_direct(near, far, sent, mine)
    kept, landed[1], landed[2], pages[3] = lax.optimization_barrier(
        (kept, landed[1], landed[2], pages[3])
    )
    landed[3] = lax.ppermute(pages[3], "attn", swap_perm(4, 3))
    came = {d: lax.ppermute(kept, "ffn", swap_perm(4, d)) for d in (2, 3, 1)}
    mixed = jnp.stack([kept, came[1], came[2], came[3]])
    mixed, landed[3] = lax.optimization_barrier((mixed, landed[3]))
    rows = mixed.reshape(count, columns)

    stages = []
    for c in range(CHUNKS):
        near, far, sent = gate_and_up(rows, w_gate, w_up, c * step, step)
        came, leaving = fold_first(sent, far, "attn")
        rows = tie(rows, leaving)
        stages.append((near, came, leaving))
    hiddens = []
    for c in range(CHUNKS):
        near, came, leaving = stages[c]
        sums = fold_last(leaving, (near, came), "attn")
        quarter = (jax.nn.silu(sums[:, :step]) * sums[:, step:]).astype(jnp.bfloat16)
        across = lax.ppermute(quarter, "attn", swap_perm(4, 2))
        if c + 1 < CHUNKS:
            across = tie(across, stages[c + 1][2])
        half = jnp.stack([quarter, across])
        other = lax.ppermute(half, "attn", swap_perm(4, 1))
        hidden = jnp.stack([half[0], other[0], half[1], other[1]]).reshape(count, step)
        hiddens.append(hidden)
    sums = down_project(position, hiddens, w_down)
    sums, landed = lax.optimization_barrier((sums, landed))
    kept = lax.dynamic_index_in_dim(mixed, position, 0, keepdims=False)
    outs = [sum_direct(*sums[0], kept)]
    return jnp.concatenate(outs, axis=1), landed


def settle(landed, incoming, pool_count, room_in, turn):
    came_usable = incoming < pool_count
    position_in = jnp.cumsum(came_usable.astype(jnp.int32)) - 1
    lanes = jnp.arange(room_in, dtype=jnp.int32)
    matches = jnp.logical_and(came_usable[None, :], position_in[None, :] == lanes[:, None])
    present = jnp.any(matches, axis=1)
    chosen = jnp.argmax(matches, axis=1)
    if turn is not None:
        pair_room = landed.shape[0] // 4
        chosen = jnp.bitwise_xor(chosen // pair_room, turn) * pair_room + chosen % pair_room
    arrived = jnp.take(landed, chosen, axis=0)
    return jnp.where(present[:, None, None], arrived, jnp.zeros_like(arrived))


def body(
    queries,
    new_kv,
    cache_pool,
    request_owner,
    block_req,
    migrate,
    residual_rows,
    w_out,
    w_gate,
    w_up,
    w_down,
):
    attn_count = lax.axis_size("attn")
    ffn_count = lax.axis_size("ffn")
    position = lax.axis_index("attn")
    ffn_position = lax.axis_index("ffn")
    req_dev = queries.shape[0]
    total_req = request_owner.shape[0]
    capacity = req_dev // 4
    slot_count = attn_count * capacity
    pool_count = cache_pool.shape[0]
    head_size = cache_pool.shape[2] // 2
    head_count = queries.shape[1] // head_size
    pair_room = migrate.shape[2]
    room_in = max(2, attn_count // 4) + 1
    paired = attn_count == 4 and ffn_count == 4

    owner_grid = request_owner.reshape(attn_count, req_dev)
    order = jnp.arange(req_dev, dtype=jnp.int32)
    earlier = order[None, :] < order[:, None]
    same = owner_grid[:, :, None] == owner_grid[:, None, :]
    order_rank = jnp.sum(jnp.logical_and(same, earlier[None]), axis=2)
    within = (jnp.arange(attn_count, dtype=jnp.int32)[:, None] * capacity + order_rank).reshape(-1)
    mine_owner = lax.dynamic_slice_in_dim(owner_grid, position, 1, 0)[0]
    mine_rank = lax.dynamic_slice_in_dim(order_rank, position, 1, 0)[0]
    target = jnp.bitwise_xor(mine_owner, position) if paired else mine_owner
    picker = (
        jnp.arange(slot_count, dtype=jnp.int32)[:, None] == (target * capacity + mine_rank)[None, :]
    ).astype(jnp.bfloat16)
    send = (
        jnp.dot(
            picker, jnp.concatenate([queries, new_kv], axis=1), preferred_element_type=jnp.float32
        )
        .astype(jnp.bfloat16)
        .reshape(attn_count, capacity, -1)
    )
    if paired:
        received = [send[0]] + [
            lax.ppermute(send[d], "attn", swap_perm(4, d)) for d in (2, 3, 1)
        ]
        distances = (0, 2, 3, 1)
    else:
        received = lax.all_to_all(send, "attn", split_axis=0, concat_axis=0, tiled=True)
        received = [received.reshape(slot_count, -1)]
        distances = (0,)
    my_moves = lax.dynamic_index_in_dim(migrate, position, 0, keepdims=False)
    numbers = jnp.concatenate(
        [
            position.astype(jnp.int32).reshape(1),
            lax.dynamic_index_in_dim(block_req, position, 0, keepdims=False),
            my_moves.reshape(-1),
            within,
        ]
    )
    attention, twin, *pages = attend(
        numbers,
        (attn_count, pair_room),
        received,
        distances,
        cache_pool,
        slot_count,
        head_count,
        head_size,
    )

    if paired:
        across = lax.ppermute(twin, "attn", swap_perm(4, 2))
        beside = lax.ppermute(twin, "attn", swap_perm(4, 1))
        corner = lax.ppermute(across, "attn", swap_perm(4, 1))
        everyone = [twin, across, beside, corner]
        distance = jnp.bitwise_xor(request_owner, position)
        place = distance // 2 + (distance % 2) * 2
    else:
        everyone = lax.all_gather(attention, "attn", axis=0, tiled=True)
        place = request_owner
    row_share = total_req // ffn_count
    row_of = (place * slot_count + within).reshape(ffn_count, row_share)
    if paired:
        turn = jnp.bitwise_xor(ffn_position, position)
        row_of = jnp.take(row_of, jnp.bitwise_xor(jnp.arange(4, dtype=jnp.int32), turn), axis=0)
    row_of = row_of.reshape(-1)
    row_picker = (
        row_of[:, None] == jnp.arange(attn_count * slot_count, dtype=jnp.int32)[None, :]
    ).astype(jnp.bfloat16)

    incoming = lax.dynamic_slice_in_dim(migrate, position, 1, 1)[:, 0, :].reshape(-1)
    if paired:
        ffn_out, landed = paired_rows(
            everyone, row_picker, residual_rows, turn, position, pages, w_out, w_gate, w_up, w_down
        )
        arrived = settle(jnp.concatenate(landed), incoming, pool_count, room_in, position)
        return (attention, arrived, ffn_out)

    sent_index = jnp.minimum(my_moves, pool_count - 1).reshape(-1)
    sent_blocks = jnp.take(cache_pool, sent_index, axis=0)
    sent_blocks = sent_blocks.reshape(attn_count, pair_room, cache_pool.shape[1], 2 * head_size)
    landed = lax.all_to_all(sent_blocks, "attn", split_axis=0, concat_axis=0, tiled=True)
    landed = landed.reshape(attn_count * pair_room, landed.shape[2], landed.shape[3])
    arrived = settle(landed, incoming, pool_count, room_in, None)

    ordered = jnp.dot(row_picker, everyone, preferred_element_type=jnp.float32).astype(jnp.bfloat16)
    columns = w_out.shape[1]
    projected = jnp.dot(ordered, w_out, preferred_element_type=jnp.float32).astype(jnp.bfloat16)
    parts = projected.reshape(ffn_count, row_share, columns)
    parts = lax.all_to_all(parts, "ffn", split_axis=0, concat_axis=0, tiled=True)
    mine = lax.dynamic_slice_in_dim(residual_rows, ffn_position * row_share, row_share, 0)
    kept = (mine.astype(jnp.float32) + jnp.sum(parts.astype(jnp.float32), axis=0)).astype(
        jnp.bfloat16
    )
    rows = lax.all_gather(kept, "ffn", axis=0, tiled=True)
    gate = jnp.dot(rows, w_gate, preferred_element_type=jnp.float32)
    up = jnp.dot(rows, w_up, preferred_element_type=jnp.float32)
    gate, up = lax.psum_scatter((gate, up), "attn", scatter_dimension=0, tiled=True)
    quarter = (jax.nn.silu(gate) * up).astype(jnp.bfloat16)
    hidden = lax.all_gather(quarter, "attn", axis=0, tiled=True)
    down = jnp.dot(hidden, w_down, preferred_element_type=jnp.float32).astype(jnp.bfloat16)
    shares = lax.all_to_all(
        down.reshape(ffn_count, row_share, columns), "ffn", split_axis=0, concat_axis=0, tiled=True
    )
    total = jnp.sum(shares.astype(jnp.float32), axis=0)
    ffn_out = (kept.astype(jnp.float32) + total).astype(jnp.bfloat16)
    return (attention, arrived, ffn_out)


def solution(mesh):
    placed = (
        P(("groups", "attn"), "ffn"),
        P(("groups", "attn"), None),
        P(("groups", "attn"), None, None),
        P("groups"),
        P("groups", None),
        P("groups", None, None),
        P("groups", "attn"),
        P("ffn", "attn"),
        P("attn", "ffn"),
        P("attn", "ffn"),
        P("ffn", "attn"),
    )
    return jax.shard_map(
        body,
        mesh=mesh,
        in_specs=placed,
        out_specs=(
            P(("groups", "attn"), "ffn"),
            P(("groups", "attn"), None, None),
            P(("groups", "ffn"), "attn"),
        ),
        check_vma=False,
    )
```
